512 devices in a mesh: rows: 128 (over y, x_lo, z), band: 4 (over x_hi, core).
Axes of the slice: x: 4 (x_hi: 2, x_lo: 2; x = x_hi * 2 + x_lo), y: 4, z: 16, core: 2. Of those that a mesh axis runs over, the one named last changes fastest.
Arguments:
- embedding: bfloat16 [16384, 512], P('rows'), may hold values from -6 to 6
- w_left: bfloat16 [512, 32], replicated, may hold values from -0.25 to 0.25
- w_right: bfloat16 [512, 32], replicated, may hold values from -0.25 to 0.25
- w_in: bfloat16 [32, 128], replicated, may hold values from -1 to 1
- w_out: bfloat16 [128, 32], replicated, may hold values from -0.5 to 0.5
- w_head: float32 [32], replicated, may hold values from -1 to 1
- dist_bias: float32 [32, 4], replicated, may hold values from -3 to 3
- offsets: int32 [128, 4], P('rows', 'band'), may hold values from 0 to 3, each once within a row
- valid_bins: int32 [16384], P('rows'), may hold values 0 or 1
- target: bfloat16 [128, 4, 128, 128], P('rows', 'band'), may hold values from -6 to 6
Outputs:
- predicted: bfloat16 [128, 4, 128, 128], P('rows', 'band')
- grad_embedding: bfloat16 [16384, 512], P('rows', 'band')
- grad_left: float32 [512, 32], replicated
- grad_right: float32 [512, 32], replicated
- grad_in: float32 [32, 128], replicated
- grad_out: float32 [128, 32], replicated
- grad_head: float32 [32], replicated
- grad_bias: float32 [32, 4], replicated
The draws below stay inside these ranges and needn't reach their ends.
Inputs may be any that keep to these rules, and one draw needn't show every extreme that they name: `offsets`: each row tile's 4 entries are the numbers 0 to 3 in some order.
All inputs are finite; a program needn't handle non-finite values. No bound on the sum of `valid_bins` on one device may be relied on, other than what follows from the above.
Results may differ from the reference program's by a relative error of at most 0.0058.
Values may be sent and summed in bfloat16 or wider, within the bound.
A program may use at most 64 MiB of HBM per device.

```python
import jax
import jax.numpy as jnp
from jax import lax

C = 512
P_SIZE = 32
HID = 128
TILE = 128
NOFF = 4
ROW_TILES = 128
BINS = 16384


def with_ends(array, own_key, smallest, top_value):
    index_at = [jax.random.randint(jax.random.fold_in(own_key, axis), (), 0, length) for axis, length in enumerate(array.shape)]
    main_axis = array.shape.index(max(array.shape))
    next_to = index_at[:main_axis] + [(index_at[main_axis] + 1) % array.shape[main_axis]] + index_at[main_axis + 1:]
    return array.at[tuple(index_at)].set(smallest).at[tuple(next_to)].set(top_value)


def block_scale(own_key, shape, pieces, least, largest):
    level, own = 1.0, jax.random.fold_in(own_key, 6)
    for axis_at, shards_of in pieces:
        heights = jnp.exp(jax.random.uniform(jax.random.fold_in(own, axis_at), (shards_of,), jnp.float32, least / len(pieces), largest / len(pieces)))
        level = level * jnp.repeat(heights, shape[axis_at] // shards_of).reshape([-1 if axis == axis_at else 1 for axis in range(len(shape))])
    return level


def gaussian(own_key, shape, width, most, split=(), held_as=jnp.bfloat16):
    drawn = width * jax.random.normal(own_key, shape, jnp.float32)
    if split:
        drawn = drawn * block_scale(own_key, shape, split, -0.22, 0.18)
    return jnp.clip(drawn, -most, most).astype(held_as)


def setup_inputs(seed: int = 0) -> dict:
    key_list = jax.random.split(jax.random.key(seed), 11)
    return {
        "embedding": gaussian(key_list[0], (BINS, C), 1.0, 6.0, ((0, 128),)),
        "w_left": gaussian(key_list[1], (C, P_SIZE), C ** -0.5, 0.25),
        "w_right": gaussian(key_list[2], (C, P_SIZE), C ** -0.5, 0.25),
        "w_in": gaussian(key_list[3], (P_SIZE, HID), P_SIZE ** -0.5, 1.0),
        "w_out": gaussian(key_list[4], (HID, P_SIZE), HID ** -0.5, 0.5),
        "w_head": gaussian(key_list[5], (P_SIZE,), P_SIZE ** -0.5, 1.0, (), jnp.float32),
        "dist_bias": gaussian(key_list[6], (P_SIZE, NOFF), 0.5, 3.0, (), jnp.float32),
        "offsets": jax.vmap(lambda own: jax.random.permutation(own, NOFF))(jax.random.split(key_list[7], ROW_TILES)).reshape((ROW_TILES, NOFF)).astype(jnp.int32),
        "valid_bins": with_ends((jax.random.randint(key_list[8], (BINS,), 0, 8) < 7).astype(jnp.int32), jax.random.fold_in(key_list[8], 1), 0, 1),
        "target": gaussian(key_list[9], (ROW_TILES, NOFF, TILE, TILE), 1.0, 6.0, ((0, 128), (1, 4))),
    }


def gelu_pair(pre_act):
    return jax.nn.gelu(pre_act, approximate=True)

def block_terms(row_proj, col_proj, bias_col, row_flags, col_flags, goal_rows, w_in, w_out, w_head):
    channels = row_proj.shape[0]
    row_count = row_proj.shape[1]
    col_count = col_proj.shape[1]
    summed = row_proj.astype(jnp.float32)[:, :, None] + col_proj.astype(jnp.float32)[:, None, :] + bias_col[:, None, None]
    summed = summed.reshape(channels, row_count * col_count)
    pair_in = summed.astype(jnp.bfloat16)
    pre_act = lax.dot_general(w_in, pair_in, (((0,), (0,)), ((), ())), preferred_element_type=jnp.float32)
    activation = gelu_pair(pre_act).astype(jnp.bfloat16)
    update = summed + lax.dot_general(w_out, activation, (((0,), (0,)), ((), ())), preferred_element_type=jnp.float32)
    logits = jnp.dot(w_head, update, precision=lax.Precision.HIGHEST)
    weight_mask = (row_flags[:, None] * col_flags[None, :]).reshape(-1)
    residual = weight_mask * (logits - goal_rows.astype(jnp.float32).reshape(-1)) / (NOFF * TILE)
    grad_update = w_head[:, None] * residual[None, :]
    grad_low = grad_update.astype(jnp.bfloat16)
    head_term = jnp.dot(update, residual, precision=lax.Precision.HIGHEST)
    out_term = lax.dot_general(activation, grad_low, (((1,), (1,)), ((), ())), preferred_element_type=jnp.float32)
    grad_act = lax.dot_general(w_out, grad_low, (((1,), (0,)), ((), ())), preferred_element_type=jnp.float32)
    _, backward = jax.vjp(gelu_pair, pre_act)
    grad_pre = backward(grad_act)[0].astype(jnp.bfloat16)
    in_term = lax.dot_general(pair_in, grad_pre, (((1,), (1,)), ((), ())), preferred_element_type=jnp.float32)
    grad_pair = grad_update + lax.dot_general(w_in, grad_pre, (((1,), (0,)), ((), ())), preferred_element_type=jnp.float32)
    grad_cube = grad_pair.reshape(channels, row_count, col_count)
    return (logits.reshape(row_count, col_count), head_term, out_term, in_term, lax.optimization_barrier(jnp.sum(grad_pair, axis=1)), lax.optimization_barrier(jnp.sum(grad_cube, axis=2)), lax.optimization_barrier(jnp.sum(grad_cube, axis=1)))

def tile_terms(row_proj, col_proj, bias_col, row_flags, col_flags, goal_tile, w_in, w_out, w_head):
    half_rows = row_proj.shape[1] // 2
    first = block_terms(row_proj[:, :half_rows], col_proj, bias_col, row_flags[:half_rows], col_flags, goal_tile[:half_rows], w_in, w_out, w_head)
    second = block_terms(row_proj[:, half_rows:], col_proj, bias_col, row_flags[half_rows:], col_flags, goal_tile[half_rows:], w_in, w_out, w_head)
    return (jnp.concatenate([first[0], second[0]], axis=0), first[1] + second[1], first[2] + second[2], first[3] + second[3], first[4] + second[4], jnp.concatenate([first[5], second[5]], axis=1), first[6] + second[6])

def project(embedding, weight):
    return lax.dot_general(weight, embedding, (((0,), (1,)), ((), ())), preferred_element_type=jnp.float32).astype(jnp.bfloat16)

def reference(embedding, w_left, w_right, w_in, w_out, w_head, dist_bias, offsets, valid_bins, target):
    left_proj = project(embedding, w_left)
    right_proj = project(embedding, w_right)
    margin = NOFF * TILE
    right_pad = jnp.pad(right_proj, ((0, 0), (0, margin)))
    flags_pad = jnp.pad(valid_bins.astype(jnp.float32), (0, margin))
    channels = w_left.shape[1]
    hidden = w_in.shape[1]
    initial = (jnp.zeros((channels, BINS), jnp.float32), jnp.zeros((channels, BINS + margin), jnp.float32), jnp.zeros((channels, hidden), jnp.float32), jnp.zeros((hidden, channels), jnp.float32), jnp.zeros((channels,), jnp.float32), jnp.zeros((channels, NOFF), jnp.float32))

    def advance(totals, item_index):
        tile_row = item_index // NOFF
        slot_index = item_index % NOFF
        offset = offsets[tile_row, slot_index]
        one_hot = (jnp.arange(NOFF, dtype=jnp.int32) == offset).astype(jnp.float32)
        bias_col = lax.optimization_barrier(jnp.sum(dist_bias * one_hot[None, :], axis=1))
        row_start = (tile_row * TILE).astype(jnp.int32)
        col_start = ((tile_row + offset) * TILE).astype(jnp.int32)
        row_proj = lax.dynamic_slice_in_dim(left_proj, row_start, TILE, 1)
        col_proj = lax.dynamic_slice_in_dim(right_pad, col_start, TILE, 1)
        row_flags = lax.dynamic_slice_in_dim(flags_pad, row_start, TILE, 0)
        col_flags = lax.dynamic_slice_in_dim(flags_pad, col_start, TILE, 0)
        goal_tile = target[tile_row, slot_index]
        logits, head_term, out_term, in_term, bias_sum, row_sums, col_sums = tile_terms(row_proj, col_proj, bias_col, row_flags, col_flags, goal_tile, w_in, w_out, w_head)
        row_acc, col_acc, in_acc, out_acc, head_acc, bias_acc = totals
        row_acc = lax.dynamic_update_slice_in_dim(row_acc, lax.dynamic_slice_in_dim(row_acc, row_start, TILE, 1) + row_sums, row_start, 1)
        col_acc = lax.dynamic_update_slice_in_dim(col_acc, lax.dynamic_slice_in_dim(col_acc, col_start, TILE, 1) + col_sums, col_start, 1)
        bias_acc = bias_acc + bias_sum[:, None] * one_hot[None, :]
        return ((row_acc, col_acc, in_acc + in_term, out_acc + out_term, head_acc + head_term, bias_acc), logits)
    totals, logits = lax.scan(advance, initial, jnp.arange(ROW_TILES * NOFF, dtype=jnp.int32))
    row_acc, col_acc, grad_in, grad_out, grad_head, grad_bias = totals
    predicted = logits.reshape(ROW_TILES, NOFF, TILE, TILE).astype(jnp.bfloat16)
    row_grad = row_acc.astype(jnp.bfloat16)
    col_grad = col_acc[:, :BINS].astype(jnp.bfloat16)
    grad_embedding = (lax.dot_general(row_grad, w_left, (((0,), (1,)), ((), ())), preferred_element_type=jnp.float32) + lax.dot_general(col_grad, w_right, (((0,), (1,)), ((), ())), preferred_element_type=jnp.float32)).astype(jnp.bfloat16)
    grad_left = lax.dot_general(embedding, row_grad, (((0,), (1,)), ((), ())), preferred_element_type=jnp.float32)
    grad_right = lax.dot_general(embedding, col_grad, (((0,), (1,)), ((), ())), preferred_element_type=jnp.float32)
    return (predicted, grad_embedding, grad_left, grad_right, grad_in, grad_out, grad_head, grad_bias)
```

```python
import functools

import jax
import jax.numpy as jnp
from jax import lax
from jax.experimental import pallas as pl
from jax.experimental.pallas import tpu as pltpu
from jax.sharding import PartitionSpec as P

TILE = 128
NOFF = 4
CH = 32
HID = 128
ROWS = 128
RING = 16
GROUPS = 8
BAND = 4
MESH = pl.DeviceIdType.MESH
F32 = jnp.float32
BF16 = jnp.bfloat16

C0 = 0.7978845608028654
C1 = C0 * 0.044715
ALPHA = C1 ** (-1.0 / 3.0)
BETA = C0 * ALPHA


def hdot(a, b, ca, cb):
    return lax.dot_general(
        a, b, (((ca,), (cb,)), ((), ())), precision=lax.Precision.HIGHEST, preferred_element_type=F32
    )


def bdot(a, b, ca, cb):
    return lax.dot_general(a, b, (((ca,), (cb,)), ((), ())), preferred_element_type=F32)


def kernel(
    off_ref, emb, wl, wr, win, wout, whead, dbias, vbins, tgt,
    pred, gemb, gl, gr, gin, gout, gex,
    abc, act, slope, b_s, v_s, gr_s, gc_s, ar_s,
    pay, pay_in, e_in,
    x_out, x_in, s_out, s_in, small,
    rs_out, rs_in, zbuf, fin, c_out, c_in,
    pay_ss, pay_rs, e_ss, e_rs, x_ss, x_rs, s_ss, s_rs, g_ss, g_rs, z_ss, z_rs, f_ss, f_rs, c_ss, c_rs,
):
    r = lax.axis_index("rows")
    b = lax.axis_index("band")
    z = lax.rem(r, RING)
    base = r - z
    g = lax.div(r, RING)

    def row_at(d):
        return lax.rem(r + (d + ROWS), ROWS)

    def ring_at(d):
        return base + lax.rem(z + d, RING)

    def group_at(d):
        return lax.rem(r + RING * d, ROWS)

    def band_at(d):
        return lax.rem(b + d, BAND)

    def remote(src, dst, ss, rs, dev):
        return pltpu.make_async_remote_copy(
            src_ref=src, dst_ref=dst, send_sem=ss, recv_sem=rs, device_id=dev, device_id_type=MESH
        )

    barrier = pltpu.get_barrier_semaphore()
    partners = [(row_at(d), b) for d in (-3, -2, -1, 1, 2, 3)]
    partners += [(ring_at(d), b) for d in range(1, RING)]
    partners += [(group_at(d), band_at(e)) for d in range(GROUPS) for e in range(BAND) if d or e]
    for dev in partners:
        pl.semaphore_signal(barrier, inc=1, device_id=dev, device_id_type=MESH)

    lt = bdot(emb[...], wl[...], 1, 0).astype(BF16)
    rt = bdot(emb[...], wr[...], 1, 0).astype(BF16)
    ltf, rtf = lt.astype(F32), rt.astype(F32)
    lr = jnp.transpose(jnp.concatenate([ltf, rtf], axis=1))
    left, right = lr[:CH], lr[CH:]
    flags = vbins[...].astype(F32)
    pay[0:CH] = right.astype(BF16)
    pay[CH:CH + 16] = jnp.broadcast_to(flags, (16, TILE)).astype(BF16)

    pl.semaphore_wait(barrier, len(partners))
    pay_c = [
        remote(pay, pay_in.at[d - 1], pay_ss.at[d - 1], pay_rs.at[d - 1], (row_at(-d), b)) for d in (3, 2, 1)
    ]
    for c in pay_c:
        c.start()

    share = pl.ds(pl.multiple_of(b * TILE, TILE), TILE)
    wh = whead[...]
    wcol = jnp.sum(
        jnp.where(
            lax.broadcasted_iota(jnp.int32, (CH, CH), 0) == lax.broadcasted_iota(jnp.int32, (CH, CH), 1), wh, 0.0
        ),
        axis=1, keepdims=True,
    )
    v_s[...] = jnp.broadcast_to(
        jnp.sum(wout[...].astype(F32) * wh, axis=1, keepdims=True), (HID, TILE)
    )
    row_logit = jnp.sum(ltf * wh, axis=1, keepdims=True)
    win_f = win[...].astype(F32)
    win_t = jnp.transpose(win_f)
    at = bdot(lt, win[...], 1, 0) * (1.0 / ALPHA)

    def spread(i, rolled):
        for j in range(8):
            abc[8 * i + j] = jnp.broadcast_to(rolled[:, j:j + 1], (TILE, TILE))
        return pltpu.roll(rolled, TILE - 8, 1)

    lax.fori_loop(0, HID // 8, spread, at)

    offset = off_ref[0, 0]
    hot = [jnp.where(offset == j, 1.0, 0.0).astype(F32) for j in range(NOFF)]
    bias_col = jnp.sum(
        jnp.where(lax.broadcasted_iota(jnp.int32, (CH, NOFF), 1) == offset, dbias[...], 0.0),
        axis=1, keepdims=True,
    )

    r_sel = right * hot[0]
    f_sel = flags * hot[0]
    for c in pay_c:
        c.wait_recv()
    for d in (1, 2, 3):
        keep = hot[d] * jnp.where(r + d < ROWS, 1.0, 0.0).astype(F32)
        r_sel = r_sel + pay_in[d - 1, 0:CH].astype(F32) * keep
        f_sel = f_sel + pay_in[d - 1, CH:CH + 16].astype(F32)[0:1] * keep

    e_c = [
        remote(emb.at[:, share], e_in.at[d - 1], e_ss.at[d - 1], e_rs.at[d - 1], (row_at(-d), b)) for d in (3, 2, 1)
    ]
    for c in e_c:
        c.start()

    r_b = r_sel + bias_col
    b_s[...] = hdot(win_t, r_b, 1, 0) * (1.0 / ALPHA)
    col_logit = jnp.sum(r_b * wcol, axis=0, keepdims=True)

    def first(i, total):
        for j in range(4):
            k = 4 * i + j
            y = abc[k] + b_s[pl.ds(k, 1), :]
            w = y * y + BETA
            t = jnp.tanh(y * w)
            q = 1.0 + t
            a2 = y * q
            act[k] = a2.astype(BF16)
            slope[k] = (q + (a2 * (1.0 - t)) * (3.0 * w - 2.0 * BETA)).astype(BF16)
            total = total + a2 * v_s[pl.ds(k, 1), :]
        return total

    total = lax.fori_loop(0, HID // 4, first, jnp.zeros((TILE, TILE), F32))
    logits = total * (0.5 * ALPHA) + (row_logit + col_logit)
    pred[...] = logits.astype(BF16)
    row_flags = jnp.sum(
        jnp.where(
            lax.broadcasted_iota(jnp.int32, (TILE, TILE), 0) == lax.broadcasted_iota(jnp.int32, (TILE, TILE), 1),
            flags, 0.0,
        ),
        axis=1, keepdims=True,
    )
    res = (row_flags * f_sel) * (logits - tgt[...].astype(F32)) * (1.0 / (NOFF * TILE))
    res_b = res.astype(BF16)
    ones = jnp.ones((8, TILE), BF16)

    def second(i, carry):
        for j in range(4):
            k = 4 * i + j
            h = slope[k] * res_b
            a = act[k] * res_b
            both = bdot(ones, jnp.concatenate([h, a], axis=1), 1, 0)
            gc_s[pl.ds(k, 1), :] = both[0:1, :TILE]
            ar_s[pl.ds(k, 1), :] = both[0:1, TILE:]
            gr_s[pl.ds(k, 1), :] = bdot(ones, h, 1, 1)[0:1]
        return carry

    lax.fori_loop(0, HID // 4, second, 0)

    ones_f = jnp.ones((8, TILE), F32)
    half_v = v_s[...] * 0.5
    g_both = jnp.concatenate([gr_s[...] * half_v, gc_s[...] * half_v], axis=1)
    rr = hdot(ones_f, res, 1, 1)
    rc = jnp.broadcast_to(jnp.sum(res, axis=0, keepdims=True), (8, TILE))
    r_both = jnp.concatenate([rr, rc], axis=1)
    p_both = jnp.concatenate([left, r_b], axis=1)
    sums = hdot(win_f, g_both, 1, 0) + wcol * r_both[0:1]
    sums_b = sums.astype(BF16)
    gin_part = hdot(p_both, g_both, 1, 1)
    head = hdot(r_both, p_both, 1, 1)
    bias = hdot(ones_f, sums[:, :TILE], 1, 1)
    ar = hdot(ones_f, ar_s[...], 1, 1)
    row_id = lax.broadcasted_iota(jnp.int32, (8, TILE), 0)
    small[...] = jnp.where(row_id == 5, ar, jnp.where(row_id == 6, offset.astype(F32), 0.0))
    for j in range(NOFF):
        small[j:j + 1, 0:CH] = bias[0:1] * hot[j]
    small[4:5, 0:CH] = head[0:1]
    extra = small[...]

    x_out[0:CH] = sums_b[:, :TILE]
    x_out[CH:2 * CH] = sums_b[:, TILE:]
    for e in range(BAND):
        s_out[e, 0:8] = gin_part[8 * e:8 * e + 8]
        s_out[e, 8:16] = extra
    x_c, s_c = [], []
    for e in (2, 3, 1):
        dev = (r, band_at(e))
        x_c.append(remote(x_out, x_in.at[e - 1], x_ss.at[e - 1], x_rs.at[e - 1], dev))
        s_c.append(remote(s_out.at[band_at(e)], s_in.at[e - 1], s_ss.at[e - 1], s_rs.at[e - 1], dev))
    for c, s in zip(x_c, s_c):
        c.start()
        s.start()
    for c in e_c:
        c.wait_recv()
    for c, s in zip(x_c, s_c):
        c.wait_recv()
        s.wait_recv()
    own = x_out[...].astype(F32)
    row_tot = own[:CH]
    cols = [own[CH:] * hot[j] for j in range(NOFF)]
    mine = s_out[b]
    for e in range(BAND - 1):
        got = x_in[e].astype(F32)
        its = s_in[e]
        row_tot = row_tot + got[:CH]
        its_offset = its[14:15, :]
        for j in range(NOFF):
            cols[j] = cols[j] + jnp.where(its_offset == j, got[CH:], 0.0)
        mine = mine + its
    row_b = row_tot.astype(BF16)
    cols_b = [c.astype(BF16) for c in cols]
    part_l = bdot(row_b, emb[:, share], 1, 0)
    part_r = bdot(cols_b[0], emb[:, share], 1, 0)
    for d in (1, 2, 3):
        part_r = part_r + bdot(cols_b[d], e_in[d - 1], 1, 0)
    for j in range(4):
        rs_out[j, 0:8] = part_l[8 * j:8 * j + 8]
        rs_out[4 + j, 0:8] = part_r[8 * j:8 * j + 8]
    zero = jnp.zeros((6, TILE), F32)
    for j in range(GROUPS):
        rs_out[j, 8:16] = jnp.concatenate([mine[j:j + 1], mine[8 + j:9 + j], zero], axis=0)

    g_c = [
        remote(
            rs_out.at[lax.rem(g + d, GROUPS)], rs_in.at[d - 1], g_ss.at[d - 1], g_rs.at[d - 1], (group_at(d), b)
        )
        for d in (5, 3, 4, 6, 2, 7, 1)
    ]
    for c in g_c:
        c.start()
    for d in (1, 2, 3):
        c_out[d - 1] = cols_b[d]
    c_c = [
        remote(c_out.at[d - 1], c_in.at[d - 1], c_ss.at[d - 1], c_rs.at[d - 1], (row_at(d), b)) for d in (3, 2, 1)
    ]
    for c in c_c:
        c.start()
    mine = rs_out[g]
    for c in g_c:
        c.wait_recv()
    for d in range(GROUPS - 1):
        mine = mine + rs_in[d]
    zbuf[z] = mine.astype(BF16)

    z_c = [
        remote(
            zbuf.at[z], zbuf.at[z], z_ss.at[d - 1], z_rs.at[z], (ring_at(d), b)
        )
        for d in (8, 7, 9, 6, 10, 5, 11, 4, 12, 3, 13, 2, 14, 1, 15)
    ]
    for c in z_c:
        c.start()

    for c in c_c:
        c.wait_recv()
    col_tot = cols[0]
    for d in (1, 2, 3):
        col_tot = col_tot + c_in[d - 1].astype(F32)
    both_t = jnp.transpose(jnp.concatenate([row_tot, col_tot], axis=0)).astype(BF16)
    w_both = jnp.concatenate([wl[share, :], wr[share, :]], axis=1)
    gemb[...] = bdot(both_t, w_both, 1, 1).astype(BF16)

    for d in range(1, RING):
        at_z = lax.rem(z + d, RING)
        remote(zbuf.at[z], zbuf.at[at_z], z_ss.at[d - 1], z_rs.at[at_z], (ring_at(d), b)).wait_recv()
    whole = zbuf[0].astype(F32)
    for d in range(1, RING):
        whole = whole + zbuf[d].astype(F32)
    me = g * BAND + b
    fin[me] = whole.astype(BF16)

    order = [(d, e) for d in range(GROUPS) for e in range(BAND) if d or e]
    f_c = []
    for n, (d, e) in enumerate(order):
        f_c.append(remote(fin.at[me], fin.at[me], f_ss.at[n], f_rs.at[me], (group_at(d), band_at(e))))
    for c in f_c:
        c.start()
    for n, (d, e) in enumerate(order):
        src = lax.rem(g + d, GROUPS) * BAND + band_at(e)
        remote(fin.at[me], fin.at[src], f_ss.at[n], f_rs.at[src], (group_at(d), band_at(e))).wait_recv()
    for j in range(GROUPS):
        out = gl if j < 4 else gr
        for e in range(BAND):
            chunk = fin[j * BAND + e].astype(F32)
            out[8 * (j % 4):8 * (j % 4) + 8, TILE * e:TILE * (e + 1)] = chunk[0:8]
            gin[8 * e + j:8 * e + j + 1, :] = chunk[8:9]
            if e == 0:
                small[j:j + 1, :] = chunk[9:10]
    ar_row = small[5:6, :] * (0.5 * ALPHA)
    ar_8 = jnp.where(row_id == 0, jnp.broadcast_to(ar_row, (8, TILE)), 0.0)
    ar_col = jnp.transpose(jnp.broadcast_to(ar_row, (TILE, TILE)))
    gout[...] = ar_col[:, :CH] * wh
    gex[...] = small[...]
    gex[4:5, 0:CH] = small[4:5, 0:CH] + hdot(ar_8, wout[...].astype(F32), 1, 0)[0:1]

    for c in pay_c + e_c + x_c + s_c + g_c + c_c + z_c + f_c:
        c.wait_send()


def on_device(emb, wl, wr, win, wout, whead, dbias, offsets, vbins, target):
    vm = pl.BlockSpec(memory_space=pltpu.VMEM)
    sd = jax.ShapeDtypeStruct
    dma = pltpu.SemaphoreType.DMA
    outs = pl.pallas_call(
        kernel,
        out_shape=(
            sd((TILE, TILE), BF16), sd((TILE, TILE), BF16), sd((CH, 512), F32), sd((CH, 512), F32),
            sd((CH, HID), F32), sd((HID, CH), F32), sd((8, TILE), F32),
        ),
        in_specs=[pl.BlockSpec(memory_space=pltpu.SMEM)] + [vm] * 9,
        out_specs=(vm,) * 7,
        scratch_shapes=[
            pltpu.VMEM((HID, TILE, TILE), F32),
            pltpu.VMEM((HID, TILE, TILE), BF16),
            pltpu.VMEM((HID, TILE, TILE), BF16),
            pltpu.VMEM((HID, TILE), F32),
            pltpu.VMEM((HID, TILE), F32),
            pltpu.VMEM((HID, TILE), F32),
            pltpu.VMEM((HID, TILE), F32),
            pltpu.VMEM((HID, TILE), F32),
            pltpu.VMEM((48, TILE), BF16),
            pltpu.VMEM((3, 48, TILE), BF16),
            pltpu.VMEM((3, TILE, TILE), BF16),
            pltpu.VMEM((2 * CH, TILE), BF16),
            pltpu.VMEM((3, 2 * CH, TILE), BF16),
            pltpu.VMEM((BAND, 16, TILE), F32),
            pltpu.VMEM((3, 16, TILE), F32),
            pltpu.VMEM((8, TILE), F32),
            pltpu.VMEM((GROUPS, 16, TILE), F32),
            pltpu.VMEM((GROUPS - 1, 16, TILE), F32),
            pltpu.VMEM((RING, 16, TILE), BF16),
            pltpu.VMEM((GROUPS * BAND, 16, TILE), BF16),
            pltpu.VMEM((3, CH, TILE), BF16),
            pltpu.VMEM((3, CH, TILE), BF16),
            dma((3,)), dma((3,)), dma((3,)), dma((3,)), dma((3,)), dma((3,)), dma((3,)), dma((3,)),
            dma((7,)), dma((7,)), dma((15,)), dma((16,)), dma((31,)), dma((32,)), dma((3,)), dma((3,)),
        ],
        compiler_params=pltpu.CompilerParams(
            collective_id=0, has_side_effects=True, vmem_limit_bytes=48 * 1024 * 1024
        ),
        name="step",
    )(
        offsets, emb, wl, wr, win, wout, whead.reshape(1, CH), dbias, vbins.reshape(1, TILE),
        target.reshape(TILE, TILE),
    )
    pred, gemb, gl, gr, gin, gout, gex = outs
    return (
        pred.reshape(1, 1, TILE, TILE), gemb, gl.T, gr.T, gin, gout, gex[4, :CH], gex[:NOFF, :CH].T,
    )


def solution(mesh):
    return jax.shard_map(
        on_device,
        mesh=mesh,
        in_specs=(
            P("rows", None), P(), P(), P(), P(), P(), P(), P("rows", "band"), P("rows"),
            P("rows", "band", None, None),
        ),
        out_specs=(P("rows", "band", None, None), P("rows", "band"), P(), P(), P(), P(), P(), P()),
        check_vma=False,
    )
```

```python
import functools

import jax
import jax.numpy as jnp
from jax import lax
from jax.experimental import pallas as pl
from jax.experimental.pallas import tpu as pltpu
from jax.sharding import PartitionSpec as P

TILE = 128
NOFF = 4
CH = 32
HID = 128
ROWS = 128
RING = 16
GROUPS = 8
BAND = 4
MESH = pl.DeviceIdType.MESH
F32 = jnp.float32
BF16 = jnp.bfloat16

C0 = 0.7978845608028654
C1 = C0 * 0.044715
ALPHA = C1 ** (-1.0 / 3.0)
BETA = C0 * ALPHA


def hdot(a, b, ca, cb):
    return lax.dot_general(
        a, b, (((ca,), (cb,)), ((), ())), precision=lax.Precision.HIGHEST, preferred_element_type=F32
    )


def bdot(a, b, ca, cb):
    return lax.dot_general(a, b, (((ca,), (cb,)), ((), ())), preferred_element_type=F32)


def kernel(
    emb_h, wl_h, wr_h, win_h, wout_h, whead_h, dbias_h, off_h, vbins_h, tgt_h,
    pred, gemb, gl, gr, gin, gout, ghead, gbias,
    emb, wl, wr, win, wout, whead, dbias, off, vbins, tgt, load_s,
    abc, act, slope, b_s, v_s, gr_s, gc_s, ar_s,
    pay, pay_in, e_in,
    x_out, x_in, s_out, s_in, small,
    rs_out, rs_in, zbuf, fin, c_out, c_in,
    pay_ss, pay_rs, e_ss, e_rs, x_ss, x_rs, s_ss, s_rs, g_ss, g_rs, z_ss, z_rs, f_ss, f_rs, c_ss, c_rs, here,
):
    loads = [
        pltpu.make_async_copy(src, dst, load_s.at[n])
        for n, (src, dst) in enumerate(
            [
                (wr_h, wr), (emb_h, emb), (wl_h, wl), (vbins_h, vbins), (win_h, win), (wout_h, wout),
                (whead_h, whead), (dbias_h, dbias), (off_h, off), (tgt_h, tgt),
            ]
        )
    ]
    for c in loads:
        c.start()

    r = lax.axis_index("rows")
    b = lax.axis_index("band")
    z = lax.rem(r, RING)
    base = r - z
    g = lax.div(r, RING)

    def row_at(d):
        return lax.rem(r + (d + ROWS), ROWS)

    def ring_at(d):
        return base + lax.rem(z + d, RING)

    def group_at(d):
        return lax.rem(r + RING * d, ROWS)

    def band_at(d):
        return lax.rem(b + d, BAND)

    def remote(src, dst, ss, rs, dev):
        return pltpu.make_async_remote_copy(
            src_ref=src, dst_ref=dst, send_sem=ss, recv_sem=rs, device_id=dev, device_id_type=MESH
        )

    barrier = pltpu.get_barrier_semaphore()
    partners = [(row_at(d), b) for d in (-3, -2, -1, 1, 2, 3)]
    partners += [(ring_at(d), b) for d in (1, 2, 3, 4, 12, 13, 14, 15)]
    partners += [(group_at(d), band_at(e)) for d in range(GROUPS) for e in range(BAND) if d or e]
    for dev in partners:
        pl.semaphore_signal(barrier, inc=1, device_id=dev, device_id_type=MESH)

    for c in loads[:4]:
        c.wait()
    right_b = bdot(wr[...], emb[...], 1, 1).astype(BF16)
    right = right_b.astype(F32)
    flags = vbins[...].astype(F32)
    pay[0:CH] = right_b
    pay[CH:CH + 16] = jnp.broadcast_to(flags, (16, TILE)).astype(BF16)

    pl.semaphore_wait(barrier, len(partners))
    pay_c = [
        remote(pay, pay_in.at[d - 1], pay_ss.at[d - 1], pay_rs.at[d - 1], (row_at(-d), b)) for d in (3, 2, 1)
    ]
    for c in pay_c:
        c.start()
    for d in (4, 12):
        pl.semaphore_signal(here, inc=1, device_id=(ring_at(d), b), device_id_type=MESH)

    share = pl.ds(pl.multiple_of(b * TILE, TILE), TILE)
    left = bdot(wl[...], emb[...], 1, 1).astype(BF16).astype(F32)
    ltf = jnp.transpose(left)
    lt = ltf.astype(BF16)
    for c in loads[4:]:
        c.wait()
    wh = whead[...]
    wcol = jnp.sum(
        jnp.where(
            lax.broadcasted_iota(jnp.int32, (CH, CH), 0) == lax.broadcasted_iota(jnp.int32, (CH, CH), 1), wh, 0.0
        ),
        axis=1, keepdims=True,
    )
    wout_f = wout[...].astype(F32)
    v_s[...] = jnp.transpose(
        jnp.broadcast_to(jnp.sum(wout_f * wcol, axis=0, keepdims=True), (TILE, HID))
    )
    row_logit = jnp.sum(ltf * wh, axis=1, keepdims=True)
    win_f = win[...].astype(F32)
    win_t = jnp.transpose(win_f)
    at = bdot(lt, win[...], 1, 0) * (1.0 / ALPHA)

    def spread(i, rolled):
        for j in range(8):
            abc[8 * i + j] = jnp.broadcast_to(rolled[:, j:j + 1], (TILE, TILE))
        return pltpu.roll(rolled, TILE - 8, 1)

    lax.fori_loop(0, HID // 8, spread, at)

    offset = off[...]
    hot = [jnp.where(offset == j, 1.0, 0.0).astype(F32) for j in range(NOFF)]
    bias_row = sum(dbias[j:j + 1, :] * hot[j] for j in range(NOFF))
    bias_col = jnp.sum(
        jnp.where(
            lax.broadcasted_iota(jnp.int32, (CH, CH), 0) == lax.broadcasted_iota(jnp.int32, (CH, CH), 1),
            bias_row, 0.0,
        ),
        axis=1, keepdims=True,
    )

    r_sel = right * hot[0]
    f_sel = flags * hot[0]
    for c in pay_c:
        c.wait_recv()
    for d in (1, 2, 3):
        keep = hot[d] * jnp.where(r + d < ROWS, 1.0, 0.0).astype(F32)
        r_sel = r_sel + pay_in[d - 1, 0:CH].astype(F32) * keep
        f_sel = f_sel + pay_in[d - 1, CH:CH + 16].astype(F32)[0:1] * keep

    e_c = [
        remote(emb.at[:, share], e_in.at[d - 1], e_ss.at[d - 1], e_rs.at[d - 1], (row_at(-d), b)) for d in (3, 2, 1)
    ]
    for c in e_c:
        c.start()

    r_b = r_sel + bias_col
    b_s[...] = hdot(win_t, r_b, 1, 0) * (1.0 / ALPHA)
    col_logit = jnp.sum(r_b * wcol, axis=0, keepdims=True)

    def first(i, total):
        for j in range(8):
            k = 8 * i + j
            y = abc[k] + b_s[pl.ds(k, 1), :]
            w = y * y + BETA
            t = jnp.tanh(y * w)
            q = 1.0 + t
            a2 = y * q
            act[k] = a2
            slope[k] = q + (a2 * (1.0 - t)) * (3.0 * w - 2.0 * BETA)
            total = total + a2 * v_s[pl.ds(k, 1), :]
        return total

    total = lax.fori_loop(0, HID // 8, first, jnp.zeros((TILE, TILE), F32))
    logits = total * (0.5 * ALPHA) + (row_logit + col_logit)
    pred[...] = logits.astype(BF16)
    row_flags = jnp.sum(
        jnp.where(
            lax.broadcasted_iota(jnp.int32, (TILE, TILE), 0) == lax.broadcasted_iota(jnp.int32, (TILE, TILE), 1),
            flags, 0.0,
        ),
        axis=1, keepdims=True,
    )
    res = (row_flags * f_sel) * (logits - tgt[...].astype(F32)) * (1.0 / (NOFF * TILE))
    ones = jnp.ones((8, TILE), BF16)

    def second(i, carry):
        parts = []
        for j in range(16):
            k = 16 * i + j
            h = slope[k] * res
            gc_s[pl.ds(k, 1), :] = jnp.sum(h, axis=0, keepdims=True)
            ar_s[pl.ds(k, 1), :] = jnp.sum(act[k] * res, axis=0, keepdims=True)
            parts.append(h.astype(BF16))
        over_q = bdot(ones, jnp.concatenate(parts, axis=0), 1, 1)
        for j in range(16):
            gr_s[pl.ds(16 * i + j, 1), :] = over_q[0:1, TILE * j:TILE * (j + 1)]
        return carry

    lax.fori_loop(0, HID // 16, second, 0)

    ones_f = jnp.ones((8, TILE), F32)
    half_v = v_s[...] * 0.5
    g_both = jnp.concatenate([gr_s[...] * half_v, gc_s[...] * half_v], axis=1)
    rr = hdot(ones_f, res, 1, 1)
    rc = jnp.broadcast_to(jnp.sum(res, axis=0, keepdims=True), (8, TILE))
    r_both = jnp.concatenate([rr, rc], axis=1)
    p_both = jnp.concatenate([left, r_b], axis=1)
    sums = hdot(win_f, g_both, 1, 0) + wcol * r_both[0:1]
    sums_b = sums.astype(BF16)
    gin_part = hdot(p_both, g_both, 1, 1)
    head = hdot(r_both, p_both, 1, 1)
    bias = hdot(ones_f, sums[:, :TILE], 1, 1)
    ar = hdot(ones_f, ar_s[...], 1, 1)
    row_id = lax.broadcasted_iota(jnp.int32, (8, TILE), 0)
    small[...] = jnp.where(row_id == 5, ar, jnp.where(row_id == 6, offset.astype(F32), 0.0))
    for j in range(NOFF):
        small[j:j + 1, 0:CH] = bias[0:1] * hot[j]
    small[4:5, 0:CH] = head[0:1]
    extra = small[...]

    x_out[0:CH] = sums_b[:, :TILE]
    x_out[CH:2 * CH] = sums_b[:, TILE:]
    for e in range(BAND):
        s_out[e, 0:8] = gin_part[8 * e:8 * e + 8]
        s_out[e, 8:16] = extra
    x_c, s_c = [], []
    for e in (2, 3, 1):
        dev = (r, band_at(e))
        x_c.append(remote(x_out, x_in.at[e - 1], x_ss.at[e - 1], x_rs.at[e - 1], dev))
        s_c.append(remote(s_out.at[band_at(e)], s_in.at[e - 1], s_ss.at[e - 1], s_rs.at[e - 1], dev))
    for c, s in zip(x_c, s_c):
        c.start()
        s.start()
    for c in e_c:
        c.wait_recv()
    for c, s in zip(x_c, s_c):
        c.wait_recv()
        s.wait_recv()
    own = x_out[...].astype(F32)
    row_tot = own[:CH]
    cols = [own[CH:] * hot[j] for j in range(NOFF)]
    mine = s_out[b]
    for e in range(BAND - 1):
        got = x_in[e].astype(F32)
        its = s_in[e]
        row_tot = row_tot + got[:CH]
        its_offset = its[14:15, :]
        for j in range(NOFF):
            cols[j] = cols[j] + jnp.where(its_offset == j, got[CH:], 0.0)
        mine = mine + its
    row_b = row_tot.astype(BF16)
    cols_b = [c.astype(BF16) for c in cols]
    part_l = bdot(row_b, emb[:, share], 1, 0)
    part_r = bdot(cols_b[0], emb[:, share], 1, 0)
    for d in (1, 2, 3):
        part_r = part_r + bdot(cols_b[d], e_in[d - 1], 1, 0)
    for j in range(4):
        rs_out[j, 0:8] = part_l[8 * j:8 * j + 8]
        rs_out[4 + j, 0:8] = part_r[8 * j:8 * j + 8]
    zero = jnp.zeros((6, TILE), F32)
    for j in range(GROUPS):
        rs_out[j, 8:16] = jnp.concatenate([mine[j:j + 1], mine[8 + j:9 + j], zero], axis=0)

    g_c = [
        remote(
            rs_out.at[lax.rem(g + d, GROUPS)], rs_in.at[d - 1], g_ss.at[d - 1], g_rs.at[d - 1], (group_at(d), b)
        )
        for d in (5, 3, 4, 6, 2, 7, 1)
    ]
    for c in g_c:
        c.start()
    for d in (1, 2, 3):
        c_out[d - 1] = cols_b[d]
    c_c = [
        remote(c_out.at[d - 1], c_in.at[d - 1], c_ss.at[d - 1], c_rs.at[d - 1], (row_at(d), b)) for d in (3, 2, 1)
    ]
    for c in c_c:
        c.start()
    mine = rs_out[g]
    for c in g_c:
        c.wait_recv()
    for d in range(GROUPS - 1):
        mine = mine + rs_in[d]
    zbuf[z] = mine.astype(BF16)

    pl.semaphore_wait(here, 2)
    z_c = [
        remote(
            zbuf.at[z], zbuf.at[z], z_ss.at[d - 1], z_rs.at[z], (ring_at(d), b)
        )
        for d in (8, 7, 9, 6, 10, 5, 11, 4, 12, 3, 13, 2, 14, 1, 15)
    ]
    for c in z_c:
        c.start()

    for c in c_c:
        c.wait_recv()
    col_tot = cols[0]
    for d in (1, 2, 3):
        col_tot = col_tot + c_in[d - 1].astype(F32)
    both_t = jnp.transpose(jnp.concatenate([row_tot, col_tot], axis=0)).astype(BF16)
    w_both = jnp.concatenate([wl[:, share], wr[:, share]], axis=0)
    gemb[...] = bdot(both_t, w_both, 1, 0).astype(BF16)

    for d in range(1, RING):
        at_z = lax.rem(z + d, RING)
        remote(zbuf.at[z], zbuf.at[at_z], z_ss.at[d - 1], z_rs.at[at_z], (ring_at(d), b)).wait_recv()
    whole = zbuf[0].astype(F32)
    for d in range(1, RING):
        whole = whole + zbuf[d].astype(F32)
    me = g * BAND + b
    fin[me] = whole.astype(BF16)

    order = [(d, e) for d in range(GROUPS) for e in range(BAND) if d or e]
    f_c = []
    for n, (d, e) in enumerate(order):
        f_c.append(remote(fin.at[me], fin.at[me], f_ss.at[n], f_rs.at[me], (group_at(d), band_at(e))))
    for c in f_c:
        c.start()
    for n, (d, e) in enumerate(order):
        src = lax.rem(g + d, GROUPS) * BAND + band_at(e)
        remote(fin.at[me], fin.at[src], f_ss.at[n], f_rs.at[src], (group_at(d), band_at(e))).wait_recv()
    for j in range(GROUPS):
        out = gl if j < 4 else gr
        for e in range(BAND):
            chunk = fin[j * BAND + e].astype(F32)
            out[8 * (j % 4):8 * (j % 4) + 8, TILE * e:TILE * (e + 1)] = chunk[0:8]
            gin[8 * e + j:8 * e + j + 1, :] = chunk[8:9]
            if e == 0:
                small[j:j + 1, :] = chunk[9:10]
    ar_row = small[5:6, :] * (0.5 * ALPHA)
    gout[...] = wcol * ar_row
    ghead[...] = small[4:5, 0:CH] + hdot(jnp.broadcast_to(ar_row, (8, TILE)), wout_f, 1, 1)[0:1]
    gbias[...] = small[0:NOFF, 0:CH]

    for c in pay_c + e_c + x_c + s_c + g_c + c_c + z_c + f_c:
        c.wait_send()


def write_out(*refs):
    n = (len(refs) - 1) // 2
    copies = [pltpu.make_async_copy(refs[i], refs[n + i], refs[-1].at[i]) for i in range(n)]
    for c in copies:
        c.start()
    for c in copies:
        c.wait()


def on_device(emb, wl, wr, win, wout, whead, dbias, offsets, vbins, target):
    vm = pl.BlockSpec(memory_space=pltpu.VMEM)
    hbm = pl.BlockSpec(memory_space=pltpu.HBM)
    sd = jax.ShapeDtypeStruct
    dma = pltpu.SemaphoreType.DMA
    out_shape = (
        sd((TILE, TILE), BF16), sd((TILE, TILE), BF16), sd((CH, 512), F32), sd((CH, 512), F32),
        sd((CH, HID), F32), sd((CH, HID), F32), sd((1, CH), F32), sd((NOFF, CH), F32),
    )
    outs = pl.pallas_call(
        kernel,
        out_shape=out_shape,
        in_specs=[hbm] * 10,
        out_specs=(vm,) * 8,
        scratch_shapes=[
            pltpu.VMEM((TILE, 512), BF16),
            pltpu.VMEM((CH, 512), BF16),
            pltpu.VMEM((CH, 512), BF16),
            pltpu.VMEM((CH, HID), BF16),
            pltpu.VMEM((CH, HID), BF16),
            pltpu.VMEM((1, CH), F32),
            pltpu.VMEM((NOFF, CH), F32),
            pltpu.VMEM((1, 1), jnp.int32),
            pltpu.VMEM((1, TILE), jnp.int32),
            pltpu.VMEM((TILE, TILE), BF16),
            dma((10,)),
            pltpu.VMEM((HID, TILE, TILE), F32),
            pltpu.VMEM((HID, TILE, TILE), F32),
            pltpu.VMEM((HID, TILE, TILE), F32),
            pltpu.VMEM((HID, TILE), F32),
            pltpu.VMEM((HID, TILE), F32),
            pltpu.VMEM((HID, TILE), F32),
            pltpu.VMEM((HID, TILE), F32),
            pltpu.VMEM((HID, TILE), F32),
            pltpu.VMEM((48, TILE), BF16),
            pltpu.VMEM((3, 48, TILE), BF16),
            pltpu.VMEM((3, TILE, TILE), BF16),
            pltpu.VMEM((2 * CH, TILE), BF16),
            pltpu.VMEM((3, 2 * CH, TILE), BF16),
            pltpu.VMEM((BAND, 16, TILE), F32),
            pltpu.VMEM((3, 16, TILE), F32),
            pltpu.VMEM((8, TILE), F32),
            pltpu.VMEM((GROUPS, 16, TILE), F32),
            pltpu.VMEM((GROUPS - 1, 16, TILE), F32),
            pltpu.VMEM((RING, 16, TILE), BF16),
            pltpu.VMEM((GROUPS * BAND, 16, TILE), BF16),
            pltpu.VMEM((3, CH, TILE), BF16),
            pltpu.VMEM((3, CH, TILE), BF16),
            dma((3,)), dma((3,)), dma((3,)), dma((3,)), dma((3,)), dma((3,)), dma((3,)), dma((3,)),
            dma((7,)), dma((7,)), dma((15,)), dma((16,)), dma((31,)), dma((32,)), dma((3,)), dma((3,)),
            pltpu.SemaphoreType.REGULAR,
        ],
        compiler_params=pltpu.CompilerParams(
            collective_id=0, has_side_effects=True, vmem_limit_bytes=48 * 1024 * 1024
        ),
        name="step",
    )(
        emb, wl.T, wr.T, win, wout.T, whead.reshape(1, CH), dbias.T, offsets, vbins.reshape(1, TILE),
        target.reshape(TILE, TILE),
    )
    pred, gemb, gl, gr, gin, gout, ghead, gbias = pl.pallas_call(
        write_out,
        out_shape=out_shape,
        in_specs=[vm] * 8,
        out_specs=(hbm,) * 8,
        scratch_shapes=[dma((8,))],
        compiler_params=pltpu.CompilerParams(vmem_limit_bytes=1024 * 1024),
        name="write_out",
    )(*outs)
    return (
        pred.reshape(1, 1, TILE, TILE), gemb, gl.T, gr.T, gin, gout.T, ghead.reshape(CH), gbias.T,
    )


def solution(mesh):
    return jax.shard_map(
        on_device,
        mesh=mesh,
        in_specs=(
            P("rows", None), P(), P(), P(), P(), P(), P(), P("rows", "band"), P("rows"),
            P("rows", "band", None, None),
        ),
        out_specs=(P("rows", "band", None, None), P("rows", "band"), P(), P(), P(), P(), P(), P()),
        check_vma=False,
    )
```

```python
import functools

import jax
import jax.numpy as jnp
from jax import lax
from jax.experimental import pallas as pl
from jax.experimental.pallas import tpu as pltpu
from jax.sharding import PartitionSpec as P

TILE = 128
NOFF = 4
CH = 32
HID = 128
ROWS = 128
RING = 16
GROUPS = 8
BAND = 4
GROUP_OFFSETS = ((2, 1), (2, 0), (1, 1), (3, 1), (1, 0), (3, 0), (0, 1))
BAND_OFFSETS = ((1, 1), (1, 0), (0, 1))
ALL_OFFSETS = sorted(
    (
        (dy, dx, dh, dc)
        for dy in range(4) for dx in range(2) for dh in range(2) for dc in range(2)
        if dy or dx or dh or dc
    ),
    key=lambda o: (-min(o[0], 4 - o[0]) - (1 if o[1] else 2 * o[2]), -o[3]),
)
MESH = pl.DeviceIdType.MESH
F32 = jnp.float32
BF16 = jnp.bfloat16

C0 = 0.7978845608028654
C1 = C0 * 0.044715
ALPHA = C1 ** (-1.0 / 3.0)
BETA = C0 * ALPHA


def hdot(a, b, ca, cb):
    return lax.dot_general(
        a, b, (((ca,), (cb,)), ((), ())), precision=lax.Precision.HIGHEST, preferred_element_type=F32
    )


def bdot(a, b, ca, cb):
    return lax.dot_general(a, b, (((ca,), (cb,)), ((), ())), preferred_element_type=F32)


def halves(x):
    hi = x.astype(BF16)
    return hi, (x - hi.astype(F32)).astype(BF16)


def kernel(
    emb_h, wl_h, wr_h, win_h, wout_h, whead_h, dbias_h, off_h, vbins_h, tgt_h,
    pred, gemb, gl, gr, gin, gout, ghead, gbias,
    emb, wl, wr, win, wout, whead, dbias, vbins, tgt, load_s,
    abc, act, slope, b_s, v_s, gr_s, gc_s, ar_s,
    pay, pay_in, e_in,
    x_out, x_in, s_out, s_in, small,
    rs_out, rs_in, zbuf, fin, c_out, c_in,
    pay_ss, pay_rs, e_ss, e_rs, x_ss, x_rs, s_ss, s_rs, g_ss, g_rs, z_ss, z_rs, f_ss, f_rs, c_ss, c_rs, here, there,
):
    r = lax.axis_index("rows")
    b = lax.axis_index("band")
    z = lax.rem(r, RING)
    base = r - z
    g = lax.div(r, RING)
    gy, gx = lax.div(g, 2), lax.rem(g, 2)
    bh, bc = lax.div(b, 2), lax.rem(b, 2)

    def row_at(d):
        return lax.rem(r + (d + ROWS), ROWS)

    def ring_at(d):
        return base + lax.rem(z + d, RING)

    def group_index(dy, dx):
        return lax.rem(gy + dy, 4) * 2 + lax.rem(gx + dx, 2)

    def group_at(dy, dx):
        return group_index(dy, dx) * RING + z

    def band_at(dh, dc):
        return lax.rem(bh + dh, 2) * 2 + lax.rem(bc + dc, 2)

    def signal(sem, dev):
        pl.semaphore_signal(sem, inc=1, device_id=dev, device_id_type=MESH)

    def remote(src, dst, ss, rs, dev):
        return pltpu.make_async_remote_copy(
            src_ref=src, dst_ref=dst, send_sem=ss, recv_sem=rs, device_id=dev, device_id_type=MESH
        )

    barrier = pltpu.get_barrier_semaphore()
    near = [(row_at(d), b) for d in (-3, 3, -2, 2, -1, 1)]
    for dev in near:
        signal(barrier, dev)
    loads = [
        pltpu.make_async_copy(src, dst, load_s.at[n])
        for n, (src, dst) in enumerate(
            [
                (wr_h, wr), (emb_h, emb), (wl_h, wl), (vbins_h, vbins), (win_h, win), (wout_h, wout),
                (whead_h, whead), (dbias_h, dbias), (tgt_h, tgt),
            ]
        )
    ]
    for c in loads:
        c.start()
    rest = [(group_at(dy, dx), b) for dy, dx in GROUP_OFFSETS]
    rest += [(r, band_at(dh, dc)) for dh, dc in BAND_OFFSETS]
    rest += [(ring_at(d), b) for d in (2, 14, 1, 15)]
    for dev in rest:
        signal(barrier, dev)

    for c in loads[:4]:
        c.wait()
    right_b = bdot(wr[...], emb[...], 1, 1).astype(BF16)
    right = right_b.astype(F32)
    flags = vbins[...].astype(F32)
    pay[0:CH] = right_b
    pay[CH:CH + 16] = jnp.broadcast_to(flags, (16, TILE)).astype(BF16)

    pl.semaphore_wait(barrier, len(near) + len(rest))
    pay_c = [
        remote(pay, pay_in.at[d - 1], pay_ss.at[d - 1], pay_rs.at[d - 1], (row_at(-d), b)) for d in (3, 2, 1)
    ]
    for c in pay_c:
        c.start()
    for dy, dx in GROUP_OFFSETS:
        signal(here, (group_at(dy, dx), b))
    for d in (2, 14):
        signal(here, (ring_at(d), b))

    share = pl.ds(pl.multiple_of(b * TILE, TILE), TILE)
    left = bdot(wl[...], emb[...], 1, 1).astype(BF16).astype(F32)
    ltf = jnp.transpose(left)
    lt = ltf.astype(BF16)
    for c in loads[4:]:
        c.wait()
    wh = whead[...]
    eye = lax.broadcasted_iota(jnp.int32, (CH, CH), 0) == lax.broadcasted_iota(jnp.int32, (CH, CH), 1)
    wcol = jnp.sum(jnp.where(eye, wh, 0.0), axis=1, keepdims=True)
    wout_f = wout[...].astype(F32)
    win_f = win[...].astype(F32)
    win_t = jnp.transpose(win_f)
    v_row = jnp.sum(wout_f * wcol, axis=0, keepdims=True)
    v_s[...] = jnp.transpose(jnp.broadcast_to(v_row, (TILE, HID)))
    wcol_lin = wcol + 0.5 * jnp.sum(win_f * v_row, axis=1, keepdims=True)
    wrow_lin = jnp.sum(jnp.where(eye, wcol_lin, 0.0), axis=0, keepdims=True)
    row_logit = jnp.sum(ltf * wrow_lin, axis=1, keepdims=True)
    offset = off_h[0, 0]
    hot = [jnp.where(offset == j, 1.0, 0.0).astype(F32) for j in range(NOFF)]
    bias_row = sum(dbias[j:j + 1, :] * hot[j] for j in range(NOFF))
    bias_col = jnp.sum(jnp.where(eye, bias_row, 0.0), axis=1, keepdims=True)
    b_s[...] = hdot(win_t, jnp.broadcast_to(bias_col, (CH, TILE)), 1, 0) * (1.0 / ALPHA)
    row_flags = jnp.sum(
        jnp.where(
            lax.broadcasted_iota(jnp.int32, (TILE, TILE), 0) == lax.broadcasted_iota(jnp.int32, (TILE, TILE), 1),
            flags, 0.0,
        ),
        axis=1, keepdims=True,
    )
    tgt_f = tgt[...].astype(F32)
    at = bdot(lt, win[...], 1, 0) * (1.0 / ALPHA)

    def spread(i, rolled):
        for j in range(8):
            abc[8 * i + j] = jnp.broadcast_to(rolled[:, j:j + 1], (TILE, TILE))
        return pltpu.roll(rolled, TILE - 8, 1)

    lax.fori_loop(0, HID // 8, spread, at)

    pl.semaphore_wait(here, len(GROUP_OFFSETS) + 2)
    for d in (4, 12):
        signal(there, (ring_at(d), b))

    r_sel = right * hot[0]
    f_sel = flags * hot[0]
    for c in pay_c:
        c.wait_recv()
    for d in (1, 2, 3):
        keep = hot[d] * jnp.where(r + d < ROWS, 1.0, 0.0).astype(F32)
        r_sel = r_sel + pay_in[d - 1, 0:CH].astype(F32) * keep
        f_sel = f_sel + pay_in[d - 1, CH:CH + 16].astype(F32)[0:1] * keep

    e_c = [
        remote(emb.at[:, share], e_in.at[d - 1], e_ss.at[d - 1], e_rs.at[d - 1], (row_at(-d), b)) for d in (3, 2, 1)
    ]
    for c in e_c:
        c.start()

    r_b = r_sel + bias_col
    b_s[...] += bdot(win_t.astype(BF16), r_sel.astype(BF16), 1, 0) * (1.0 / ALPHA)
    col_logit = jnp.sum(r_b * wcol_lin, axis=0, keepdims=True)

    def first(i, total):
        for j in range(8):
            k = 8 * i + j
            y = abc[k] + b_s[pl.ds(k, 1), :]
            w = y * y + BETA
            t = jnp.tanh(y * w)
            yt = y * t
            act[k] = yt
            slope[k] = t + (y - t * yt) * (3.0 * w - 2.0 * BETA)
            total = total + yt * v_s[pl.ds(k, 1), :]
        return total

    total = lax.fori_loop(0, HID // 8, first, jnp.zeros((TILE, TILE), F32))
    logits = total * (0.5 * ALPHA) + (row_logit + col_logit)
    pred[...] = logits.astype(BF16)
    res = (row_flags * f_sel) * (logits - tgt_f) * (1.0 / (NOFF * TILE))
    ones = jnp.ones((8, TILE), BF16)

    def second(i, carry):
        parts = []
        for j in range(32):
            k = 32 * i + j
            h = slope[k] * res
            gc_s[pl.ds(k, 1), :] = jnp.sum(h, axis=0, keepdims=True)
            ar_s[pl.ds(k, 1), :] = jnp.sum(act[k] * res, axis=0, keepdims=True)
            parts.append(h.astype(BF16))
        over_q = bdot(ones, jnp.concatenate(parts, axis=0), 1, 1)
        for j in range(32):
            gr_s[pl.ds(32 * i + j, 1), :] = over_q[0:1, TILE * j:TILE * (j + 1)]
        return carry

    lax.fori_loop(0, HID // 32, second, 0)

    half_v = v_s[...] * 0.5
    res_hi, res_lo = halves(res)
    rr = bdot(jnp.ones((8, 2 * TILE), BF16), jnp.concatenate([res_hi, res_lo], axis=1), 1, 1)
    rc = jnp.broadcast_to(jnp.sum(res, axis=0, keepdims=True), (8, TILE))
    r_both = jnp.concatenate([rr, rc], axis=1)
    g_both = jnp.concatenate([(gr_s[...] + rr[0:1]) * half_v, (gc_s[...] + rc[0:1]) * half_v], axis=1)
    g_hi, g_lo = halves(g_both)
    sums = wcol * r_both[0:1] + bdot(
        jnp.concatenate([win[...], win[...]], axis=1), jnp.concatenate([g_hi, g_lo], axis=0), 1, 0
    )
    sums_b = sums.astype(BF16)

    x_out[0:CH] = sums_b[:, :TILE]
    x_out[CH:2 * CH] = sums_b[:, TILE:]
    x_c, s_c = [], []
    for n, (dh, dc) in enumerate(BAND_OFFSETS):
        dev = (r, band_at(dh, dc))
        x_c.append(remote(x_out, x_in.at[n], x_ss.at[n], x_rs.at[n], dev))
        s_c.append(remote(s_out.at[band_at(dh, dc)], s_in.at[n], s_ss.at[n], s_rs.at[n], dev))
    for c in x_c:
        c.start()
    p_both = jnp.concatenate([left, r_b], axis=1)
    gin_part = hdot(p_both, g_both, 1, 1)
    head = hdot(r_both, p_both, 1, 1)
    ones_f = jnp.ones((8, TILE), F32)
    bias = hdot(ones_f, sums[:, :TILE], 1, 1)
    ar = hdot(ones_f, ar_s[...], 1, 1) + hdot(head, win_f, 1, 0) * (1.0 / ALPHA)
    row_id = lax.broadcasted_iota(jnp.int32, (8, TILE), 0)
    small[...] = jnp.where(row_id == 5, ar, jnp.where(row_id == 6, offset.astype(F32), 0.0))
    for j in range(NOFF):
        small[j:j + 1, 0:CH] = bias[0:1] * hot[j]
    small[4:5, 0:CH] = head[0:1]
    extra = small[...]
    for e in range(BAND):
        s_out[e, 0:8] = gin_part[8 * e:8 * e + 8]
        s_out[e, 8:16] = extra
    for c in s_c:
        c.start()
    for c in e_c:
        c.wait_recv()
    for c, s in zip(x_c, s_c):
        c.wait_recv()
        s.wait_recv()
    own = x_out[...].astype(F32)
    row_tot = own[:CH]
    cols = [own[CH:] * hot[j] for j in range(NOFF)]
    mine = s_out[b]
    for e in range(BAND - 1):
        got = x_in[e].astype(F32)
        its = s_in[e]
        row_tot = row_tot + got[:CH]
        its_offset = its[14:15, :]
        for j in range(NOFF):
            cols[j] = cols[j] + jnp.where(its_offset == j, got[CH:], 0.0)
        mine = mine + its
    row_b = row_tot.astype(BF16)
    cols_b = [c.astype(BF16) for c in cols]
    part_l = bdot(row_b, emb[:, share], 1, 0)
    part_r = bdot(cols_b[0], emb[:, share], 1, 0)
    for d in (1, 2, 3):
        part_r = part_r + bdot(cols_b[d], e_in[d - 1], 1, 0)
    for j in range(4):
        rs_out[j, 0:8] = part_l[8 * j:8 * j + 8]
        rs_out[4 + j, 0:8] = part_r[8 * j:8 * j + 8]
    zero = jnp.zeros((6, TILE), F32)
    for j in range(GROUPS):
        rs_out[j, 8:16] = jnp.concatenate([mine[j:j + 1], mine[8 + j:9 + j], zero], axis=0)

    g_c = [
        remote(
            rs_out.at[group_index(dy, dx)], rs_in.at[n], g_ss.at[n], g_rs.at[n], (group_at(dy, dx), b)
        )
        for n, (dy, dx) in enumerate(GROUP_OFFSETS)
    ]
    for c in g_c:
        c.start()
    for d in (1, 2, 3):
        c_out[d - 1] = cols_b[d]
    c_c = [
        remote(c_out.at[d - 1], c_in.at[d - 1], c_ss.at[d - 1], c_rs.at[d - 1], (row_at(d), b)) for d in (3, 2, 1)
    ]
    for c in c_c:
        c.start()
    mine = rs_out[g]
    for c in g_c:
        c.wait_recv()
    for d in range(GROUPS - 1):
        mine = mine + rs_in[d]
    zbuf[z] = mine.astype(BF16)

    pl.semaphore_wait(there, 2)
    z_c = [
        remote(
            zbuf.at[z], zbuf.at[z], z_ss.at[d - 1], z_rs.at[z], (ring_at(d), b)
        )
        for d in (8, 7, 9, 6, 10, 5, 11, 4, 12, 3, 13, 2, 14, 1, 15)
    ]
    for c in z_c:
        c.start()

    for c in c_c:
        c.wait_recv()
    col_tot = cols[0]
    for d in (1, 2, 3):
        col_tot = col_tot + c_in[d - 1].astype(F32)
    both_t = jnp.transpose(jnp.concatenate([row_tot, col_tot], axis=0)).astype(BF16)
    w_both = jnp.concatenate([wl[:, share], wr[:, share]], axis=0)
    gemb[...] = bdot(both_t, w_both, 1, 0).astype(BF16)

    for d in range(1, RING):
        at_z = lax.rem(z + d, RING)
        remote(zbuf.at[z], zbuf.at[at_z], z_ss.at[d - 1], z_rs.at[at_z], (ring_at(d), b)).wait_recv()
    whole = zbuf[0].astype(F32)
    for d in range(1, RING):
        whole = whole + zbuf[d].astype(F32)
    me = g * BAND + b
    fin[me] = whole.astype(BF16)

    f_c = [
        remote(fin.at[me], fin.at[me], f_ss.at[n], f_rs.at[me], (group_at(dy, dx), band_at(dh, dc)))
        for n, (dy, dx, dh, dc) in enumerate(ALL_OFFSETS)
    ]
    for c in f_c:
        c.start()
    for n, (dy, dx, dh, dc) in reversed(list(enumerate(ALL_OFFSETS))):
        src = group_index(dy, dx) * BAND + band_at(dh, dc)
        remote(
            fin.at[me], fin.at[src], f_ss.at[n], f_rs.at[src], (group_at(dy, dx), band_at(dh, dc))
        ).wait_recv()
    for j in range(GROUPS):
        out = gl if j < 4 else gr
        for e in range(BAND):
            chunk = fin[j * BAND + e].astype(F32)
            out[8 * (j % 4):8 * (j % 4) + 8, TILE * e:TILE * (e + 1)] = chunk[0:8]
            gin[8 * e + j:8 * e + j + 1, :] = chunk[8:9]
            if e == 0:
                small[j:j + 1, :] = chunk[9:10]
    ar_row = small[5:6, :] * (0.5 * ALPHA)
    gout[...] = wcol * ar_row
    ghead[...] = small[4:5, 0:CH] + hdot(jnp.broadcast_to(ar_row, (8, TILE)), wout_f, 1, 1)[0:1]
    gbias[...] = small[0:NOFF, 0:CH]

    for c in pay_c + e_c + x_c + s_c + g_c + c_c + z_c + f_c:
        c.wait_send()


def write_out(*refs):
    n = (len(refs) - 1) // 2
    copies = [pltpu.make_async_copy(refs[i], refs[n + i], refs[-1].at[i]) for i in range(n)]
    for c in copies:
        c.start()
    for c in copies:
        c.wait()


def on_device(emb, wl, wr, win, wout, whead, dbias, offsets, vbins, target):
    def keep(x):
        return pltpu.with_memory_space_constraint(x, pltpu.HBM)

    vm = pl.BlockSpec(memory_space=pltpu.VMEM)
    hbm = pl.BlockSpec(memory_space=pltpu.HBM)
    sd = jax.ShapeDtypeStruct
    dma = pltpu.SemaphoreType.DMA
    out_shape = (
        sd((TILE, TILE), BF16), sd((TILE, TILE), BF16), sd((CH, 512), F32), sd((CH, 512), F32),
        sd((CH, HID), F32), sd((CH, HID), F32), sd((1, CH), F32), sd((NOFF, CH), F32),
    )
    outs = pl.pallas_call(
        kernel,
        out_shape=out_shape,
        in_specs=[hbm] * 7 + [pl.BlockSpec(memory_space=pltpu.SMEM)] + [hbm] * 2,
        out_specs=(vm,) * 8,
        scratch_shapes=[
            pltpu.VMEM((TILE, 512), BF16),
            pltpu.VMEM((CH, 512), BF16),
            pltpu.VMEM((CH, 512), BF16),
            pltpu.VMEM((CH, HID), BF16),
            pltpu.VMEM((CH, HID), BF16),
            pltpu.VMEM((1, CH), F32),
            pltpu.VMEM((NOFF, CH), F32),
            pltpu.VMEM((1, TILE), jnp.int32),
            pltpu.VMEM((TILE, TILE), BF16),
            dma((9,)),
            pltpu.VMEM((HID, TILE, TILE), F32),
            pltpu.VMEM((HID, TILE, TILE), F32),
            pltpu.VMEM((HID, TILE, TILE), F32),
            pltpu.VMEM((HID, TILE), F32),
            pltpu.VMEM((HID, TILE), F32),
            pltpu.VMEM((HID, TILE), F32),
            pltpu.VMEM((HID, TILE), F32),
            pltpu.VMEM((HID, TILE), F32),
            pltpu.VMEM((48, TILE), BF16),
            pltpu.VMEM((3, 48, TILE), BF16),
            pltpu.VMEM((3, TILE, TILE), BF16),
            pltpu.VMEM((2 * CH, TILE), BF16),
            pltpu.VMEM((3, 2 * CH, TILE), BF16),
            pltpu.VMEM((BAND, 16, TILE), F32),
            pltpu.VMEM((3, 16, TILE), F32),
            pltpu.VMEM((8, TILE), F32),
            pltpu.VMEM((GROUPS, 16, TILE), F32),
            pltpu.VMEM((GROUPS - 1, 16, TILE), F32),
            pltpu.VMEM((RING, 16, TILE), BF16),
            pltpu.VMEM((GROUPS * BAND, 16, TILE), BF16),
            pltpu.VMEM((3, CH, TILE), BF16),
            pltpu.VMEM((3, CH, TILE), BF16),
            dma((3,)), dma((3,)), dma((3,)), dma((3,)), dma((3,)), dma((3,)), dma((3,)), dma((3,)),
            dma((7,)), dma((7,)), dma((15,)), dma((16,)), dma((31,)), dma((32,)), dma((3,)), dma((3,)),
            pltpu.SemaphoreType.REGULAR, pltpu.SemaphoreType.REGULAR,
        ],
        compiler_params=pltpu.CompilerParams(
            collective_id=0, has_side_effects=True, vmem_limit_bytes=48 * 1024 * 1024
        ),
        name="step",
    )(
        keep(emb), keep(wl.T), keep(wr.T), keep(win), keep(wout.T), keep(whead.reshape(1, CH)), keep(dbias.T),
        offsets, keep(vbins.reshape(1, TILE)), keep(target.reshape(TILE, TILE)),
    )
    pred, gemb, gl, gr, gin, gout, ghead, gbias = pl.pallas_call(
        write_out,
        out_shape=out_shape,
        in_specs=[vm] * 8,
        out_specs=(hbm,) * 8,
        scratch_shapes=[dma((8,))],
        compiler_params=pltpu.CompilerParams(vmem_limit_bytes=1024 * 1024),
        name="write_out",
    )(*outs)
    return (
        pred.reshape(1, 1, TILE, TILE), gemb, gl.T, gr.T, gin, gout.T, ghead.reshape(CH), gbias.T,
    )


def solution(mesh):
    return jax.shard_map(
        on_device,
        mesh=mesh,
        in_specs=(
            P("rows", None), P(), P(), P(), P(), P(), P(), P("rows", "band"), P("rows"),
            P("rows", "band", None, None),
        ),
        out_specs=(P("rows", "band", None, None), P("rows", "band"), P(), P(), P(), P(), P(), P()),
        check_vma=False,
    )
```

```python
import functools

import jax
import jax.numpy as jnp
from jax import lax
from jax.experimental import pallas as pl
from jax.experimental.pallas import tpu as pltpu
from jax.sharding import PartitionSpec as P

TILE = 128
NOFF = 4
CH = 32
HID = 128
ROWS = 128
RING = 16
GROUPS = 8
BAND = 4
GROUP_OFFSETS = ((2, 1), (2, 0), (1, 1), (3, 1), (1, 0), (3, 0), (0, 1))
BAND_OFFSETS = ((1, 1), (1, 0), (0, 1))
ALL_OFFSETS = sorted(
    (
        (dy, dx, dh, dc)
        for dy in range(4) for dx in range(2) for dh in range(2) for dc in range(2)
        if dy or dx or dh or dc
    ),
    key=lambda o: (-min(o[0], 4 - o[0]) - (1 if o[1] else 2 * o[2]), -o[3]),
)
MESH = pl.DeviceIdType.MESH
F32 = jnp.float32
BF16 = jnp.bfloat16

C0 = 0.7978845608028654
C1 = C0 * 0.044715
ALPHA = C1 ** (-1.0 / 3.0)
BETA = C0 * ALPHA


def hdot(a, b, ca, cb):
    return lax.dot_general(
        a, b, (((ca,), (cb,)), ((), ())), precision=lax.Precision.HIGHEST, preferred_element_type=F32
    )


def bdot(a, b, ca, cb):
    return lax.dot_general(a, b, (((ca,), (cb,)), ((), ())), preferred_element_type=F32)


def halves(x):
    hi = x.astype(BF16)
    return hi, (x - hi.astype(F32)).astype(BF16)


def kernel(
    emb_h, wl_h, wr_h, win_h, wout_h, whead_h, dbias_h, off_h, vbins_h, tgt_h,
    pred, gemb, gl, gr, gin, gout, ghead, gbias,
    emb, wl, wr, win, wout, whead, dbias, vbins, tgt, load_s,
    abc, act, slope, b_s, v_s, gr_s, gc_s, ar_s,
    pay, pay_in, flag_out, flag_in, off_out, off_in, e_in,
    x_out, x_in, s_out, s_in, small,
    rs_out, rs_in, zbuf, fin, c_out, c_in,
    pay_ss, pay_rs, flag_ss, flag_rs, off_ss, off_rs, e_ss, e_rs, x_ss, x_rs, s_ss, s_rs, g_ss, g_rs, z_ss, z_rs, f_ss, f_rs, c_ss, c_rs, here, there,
):
    r = lax.axis_index("rows")
    b = lax.axis_index("band")
    z = lax.rem(r, RING)
    base = r - z
    g = lax.div(r, RING)
    gy, gx = lax.div(g, 2), lax.rem(g, 2)
    bh, bc = lax.div(b, 2), lax.rem(b, 2)

    def row_at(d):
        return lax.rem(r + (d + ROWS), ROWS)

    def ring_at(d):
        return base + lax.rem(z + d, RING)

    def group_index(dy, dx):
        return lax.rem(gy + dy, 4) * 2 + lax.rem(gx + dx, 2)

    def group_at(dy, dx):
        return group_index(dy, dx) * RING + z

    def band_at(dh, dc):
        return lax.rem(bh + dh, 2) * 2 + lax.rem(bc + dc, 2)

    def signal(sem, dev):
        pl.semaphore_signal(sem, inc=1, device_id=dev, device_id_type=MESH)

    def remote(src, dst, ss, rs, dev):
        return pltpu.make_async_remote_copy(
            src_ref=src, dst_ref=dst, send_sem=ss, recv_sem=rs, device_id=dev, device_id_type=MESH
        )

    barrier = pltpu.get_barrier_semaphore()
    near = [(row_at(d), b) for d in (-3, 3, -2, 2, -1, 1)]
    for dev in near:
        signal(barrier, dev)
    loads = [
        pltpu.make_async_copy(src, dst, load_s.at[n])
        for n, (src, dst) in enumerate(
            [
                (wr_h, wr), (emb_h, emb), (wl_h, wl), (vbins_h, vbins), (win_h, win), (wout_h, wout),
                (whead_h, whead), (dbias_h, dbias), (tgt_h, tgt),
            ]
        )
    ]
    for c in loads:
        c.start()
    rest = [(group_at(dy, dx), b) for dy, dx in GROUP_OFFSETS]
    rest += [(r, band_at(dh, dc)) for dh, dc in BAND_OFFSETS]
    rest += [(ring_at(d), b) for d in (2, 14, 1, 15)]
    for dev in rest:
        signal(barrier, dev)

    for c in loads[:4]:
        c.wait()
    right_b = bdot(wr[...], emb[...], 1, 1).astype(BF16)
    right = right_b.astype(F32)
    flags = vbins[...].astype(F32)
    pay[...] = right_b
    flag_out[...] = jnp.broadcast_to(flags, (16, TILE)).astype(BF16)

    pl.semaphore_wait(barrier, len(near) + len(rest))
    pay_c = [
        remote(pay, pay_in.at[d - 1], pay_ss.at[d - 1], pay_rs.at[d - 1], (row_at(-d), b)) for d in (3, 2, 1)
    ]
    for c in pay_c:
        c.start()
    flag_c = [
        remote(flag_out, flag_in.at[d - 1], flag_ss.at[d - 1], flag_rs.at[d - 1], (row_at(-d), b)) for d in (3, 2, 1)
    ]
    offset = off_h[0, 0]
    off_out[...] = jnp.full((8, TILE), offset.astype(F32), F32)
    off_c = [
        remote(off_out, off_in.at[n], off_ss.at[n], off_rs.at[n], (r, band_at(dh, dc)))
        for n, (dh, dc) in enumerate(BAND_OFFSETS)
    ]
    for c in flag_c + off_c:
        c.start()
    for dy, dx in GROUP_OFFSETS:
        signal(here, (group_at(dy, dx), b))
    for d in (2, 14):
        signal(here, (ring_at(d), b))

    share = pl.ds(pl.multiple_of(b * TILE, TILE), TILE)
    left = bdot(wl[...], emb[...], 1, 1).astype(BF16).astype(F32)
    ltf = jnp.transpose(left)
    lt = ltf.astype(BF16)
    for c in loads[4:]:
        c.wait()
    wh = whead[...]
    eye = lax.broadcasted_iota(jnp.int32, (CH, CH), 0) == lax.broadcasted_iota(jnp.int32, (CH, CH), 1)
    wcol = jnp.sum(jnp.where(eye, wh, 0.0), axis=1, keepdims=True)
    wout_f = wout[...].astype(F32)
    win_f = win[...].astype(F32)
    win_t = jnp.transpose(win_f)
    v_row = jnp.sum(wout_f * wcol, axis=0, keepdims=True)
    v_s[...] = jnp.transpose(jnp.broadcast_to(v_row, (TILE, HID)))
    wcol_lin = wcol + 0.5 * jnp.sum(win_f * v_row, axis=1, keepdims=True)
    wrow_lin = jnp.sum(jnp.where(eye, wcol_lin, 0.0), axis=0, keepdims=True)
    row_logit = jnp.sum(ltf * wrow_lin, axis=1, keepdims=True)
    hot = [jnp.where(offset == j, 1.0, 0.0).astype(F32) for j in range(NOFF)]
    bias_row = sum(dbias[j:j + 1, :] * hot[j] for j in range(NOFF))
    bias_col = jnp.sum(jnp.where(eye, bias_row, 0.0), axis=1, keepdims=True)
    b_s[...] = hdot(win_t, jnp.broadcast_to(bias_col, (CH, TILE)), 1, 0) * (1.0 / ALPHA)
    row_flags = jnp.sum(
        jnp.where(
            lax.broadcasted_iota(jnp.int32, (TILE, TILE), 0) == lax.broadcasted_iota(jnp.int32, (TILE, TILE), 1),
            flags, 0.0,
        ),
        axis=1, keepdims=True,
    )
    tgt_f = tgt[...].astype(F32)
    at = bdot(lt, win[...], 1, 0) * (1.0 / ALPHA)

    def spread(i, rolled):
        for j in range(8):
            abc[8 * i + j] = jnp.broadcast_to(rolled[:, j:j + 1], (TILE, TILE))
        return pltpu.roll(rolled, TILE - 8, 1)

    lax.fori_loop(0, HID // 8, spread, at)
    for j in range(GROUPS):
        rs_out[j, 8:16] = jnp.zeros((8, TILE), F32)

    pl.semaphore_wait(here, len(GROUP_OFFSETS) + 2)
    for d in (4, 12):
        signal(there, (ring_at(d), b))

    weight = [hot[0]] + [hot[d] * jnp.where(r + d < ROWS, 1.0, 0.0).astype(F32) for d in (1, 2, 3)]
    r_sel = right * weight[0]
    for c in pay_c:
        c.wait_recv()
    for d in (1, 2, 3):
        r_sel = r_sel + pay_in[d - 1].astype(F32) * weight[d]

    e_c = [
        remote(emb.at[:, share], e_in.at[d - 1], e_ss.at[d - 1], e_rs.at[d - 1], (row_at(-d), b)) for d in (3, 2, 1)
    ]
    for c in e_c:
        c.start()

    r_b = r_sel + bias_col
    b_s[...] += bdot(win_t.astype(BF16), r_sel.astype(BF16), 1, 0) * (1.0 / ALPHA)
    col_logit = jnp.sum(r_b * wcol_lin, axis=0, keepdims=True)

    def first(i, total):
        for j in range(8):
            k = 8 * i + j
            y = abc[k] + b_s[pl.ds(k, 1), :]
            w = y * y + BETA
            t = jnp.tanh(y * w)
            yt = y * t
            act[k] = yt
            slope[k] = t + (y - t * yt) * (3.0 * w - 2.0 * BETA)
            total = total + yt * v_s[pl.ds(k, 1), :]
        return total

    total = lax.fori_loop(0, HID // 8, first, jnp.zeros((TILE, TILE), F32))
    logits = total * (0.5 * ALPHA) + (row_logit + col_logit)
    pred[...] = logits.astype(BF16)
    f_sel = flags * weight[0]
    for c in flag_c:
        c.wait_recv()
    for d in (1, 2, 3):
        f_sel = f_sel + flag_in[d - 1, 0:1].astype(F32) * weight[d]
    res = (row_flags * f_sel) * (logits - tgt_f) * (1.0 / (NOFF * TILE))
    ones = jnp.ones((8, TILE), BF16)

    parts = []
    for k in range(HID):
        h = slope[k] * res
        gc_s[k:k + 1, :] = jnp.sum(h, axis=0, keepdims=True)
        ar_s[k:k + 1, :] = jnp.sum(act[k] * res, axis=0, keepdims=True)
        parts.append(h.astype(BF16))
    over_q = bdot(ones, jnp.concatenate(parts, axis=0), 1, 1)
    for k in range(HID):
        gr_s[k:k + 1, :] = over_q[0:1, TILE * k:TILE * (k + 1)]

    half_v = v_s[...] * 0.5
    res_hi, res_lo = halves(res)
    rr = bdot(jnp.ones((8, 2 * TILE), BF16), jnp.concatenate([res_hi, res_lo], axis=1), 1, 1)
    rc = jnp.broadcast_to(jnp.sum(res, axis=0, keepdims=True), (8, TILE))
    r_both = jnp.concatenate([rr, rc], axis=1)
    g_both = jnp.concatenate([(gr_s[...] + rr[0:1]) * half_v, (gc_s[...] + rc[0:1]) * half_v], axis=1)
    g_hi, g_lo = halves(g_both)
    sums = wcol * r_both[0:1] + bdot(
        jnp.concatenate([win[...], win[...]], axis=1), jnp.concatenate([g_hi, g_lo], axis=0), 1, 0
    )
    sums_b = sums.astype(BF16)

    x_out[0:CH] = sums_b[:, :TILE]
    x_out[CH:2 * CH] = sums_b[:, TILE:]
    x_c, s_c = [], []
    for n, (dh, dc) in enumerate(BAND_OFFSETS):
        dev = (r, band_at(dh, dc))
        x_c.append(remote(x_out, x_in.at[n], x_ss.at[n], x_rs.at[n], dev))
        s_c.append(remote(s_out.at[band_at(dh, dc)], s_in.at[n], s_ss.at[n], s_rs.at[n], dev))
    for c in x_c:
        c.start()
    p_both = jnp.concatenate([left, r_b], axis=1)
    gin_part = hdot(p_both, g_both, 1, 1)
    head = hdot(r_both, p_both, 1, 1)
    ones_f = jnp.ones((8, TILE), F32)
    bias = hdot(ones_f, sums[:, :TILE], 1, 1)
    ar = hdot(ones_f, ar_s[...], 1, 1) + hdot(head, win_f, 1, 0) * (1.0 / ALPHA)
    row_id = lax.broadcasted_iota(jnp.int32, (8, TILE), 0)
    small[...] = jnp.where(row_id == 5, ar, 0.0)
    for j in range(NOFF):
        small[j:j + 1, 0:CH] = bias[0:1] * hot[j]
    small[4:5, 0:CH] = head[0:1]
    extra = small[...]
    for e in range(BAND):
        s_out[e, 0:8] = gin_part[8 * e:8 * e + 8]
        s_out[e, 8:16] = extra
    for c in s_c:
        c.start()
    for c in e_c + off_c + x_c:
        c.wait_recv()
    own = sums_b.astype(F32)
    row_tot = own[:, :TILE]
    cols = [own[:, TILE:] * hot[j] for j in range(NOFF)]
    for n in range(BAND - 1):
        got = x_in[n].astype(F32)
        row_tot = row_tot + got[:CH]
        its_offset = off_in[n, 0:1, :]
        for j in range(NOFF):
            cols[j] = cols[j] + jnp.where(its_offset == j, got[CH:], 0.0)
    row_b = row_tot.astype(BF16)
    cols_b = [c.astype(BF16) for c in cols]
    part_l = bdot(row_b, emb[:, share], 1, 0)
    part_r = bdot(cols_b[0], emb[:, share], 1, 0)
    for d in (1, 2, 3):
        part_r = part_r + bdot(cols_b[d], e_in[d - 1], 1, 0)
    for j in range(4):
        rs_out[j, 0:8] = part_l[8 * j:8 * j + 8]
        rs_out[4 + j, 0:8] = part_r[8 * j:8 * j + 8]
    mine = s_out[b]
    for c in s_c:
        c.wait_recv()
    for n in range(BAND - 1):
        mine = mine + s_in[n]
    for j in range(GROUPS):
        rs_out[j, 8:9] = mine[j:j + 1]
        rs_out[j, 9:10] = mine[8 + j:9 + j]

    g_c = [
        remote(
            rs_out.at[group_index(dy, dx)], rs_in.at[n], g_ss.at[n], g_rs.at[n], (group_at(dy, dx), b)
        )
        for n, (dy, dx) in enumerate(GROUP_OFFSETS)
    ]
    for c in g_c:
        c.start()
    for d in (1, 2, 3):
        c_out[d - 1] = cols_b[d]
    c_c = [
        remote(c_out.at[d - 1], c_in.at[d - 1], c_ss.at[d - 1], c_rs.at[d - 1], (row_at(d), b)) for d in (3, 2, 1)
    ]
    for c in c_c:
        c.start()
    mine = rs_out[g]
    for c in g_c:
        c.wait_recv()
    for d in range(GROUPS - 1):
        mine = mine + rs_in[d]
    zbuf[z] = mine.astype(BF16)

    pl.semaphore_wait(there, 2)
    z_c = [
        remote(
            zbuf.at[z], zbuf.at[z], z_ss.at[d - 1], z_rs.at[z], (ring_at(d), b)
        )
        for d in (8, 7, 9, 6, 10, 5, 11, 4, 12, 3, 13, 2, 14, 1, 15)
    ]
    for c in z_c:
        c.start()

    for c in c_c:
        c.wait_recv()
    col_tot = cols[0]
    for d in (1, 2, 3):
        col_tot = col_tot + c_in[d - 1].astype(F32)
    both_t = jnp.transpose(jnp.concatenate([row_tot, col_tot], axis=0)).astype(BF16)
    w_both = jnp.concatenate([wl[:, share], wr[:, share]], axis=0)
    gemb[...] = bdot(both_t, w_both, 1, 0).astype(BF16)

    for d in range(1, RING):
        at_z = lax.rem(z + d, RING)
        remote(zbuf.at[z], zbuf.at[at_z], z_ss.at[d - 1], z_rs.at[at_z], (ring_at(d), b)).wait_recv()
    whole = zbuf[0].astype(F32)
    for d in range(1, RING):
        whole = whole + zbuf[d].astype(F32)
    me = g * BAND + b
    fin[me] = whole.astype(BF16)

    f_c = [
        remote(fin.at[me], fin.at[me], f_ss.at[n], f_rs.at[me], (group_at(dy, dx), band_at(dh, dc)))
        for n, (dy, dx, dh, dc) in enumerate(ALL_OFFSETS)
    ]
    for c in f_c:
        c.start()
    for n, (dy, dx, dh, dc) in reversed(list(enumerate(ALL_OFFSETS))):
        src = group_index(dy, dx) * BAND + band_at(dh, dc)
        remote(
            fin.at[me], fin.at[src], f_ss.at[n], f_rs.at[src], (group_at(dy, dx), band_at(dh, dc))
        ).wait_recv()
    for j in range(GROUPS):
        out = gl if j < 4 else gr
        for e in range(BAND):
            chunk = fin[j * BAND + e].astype(F32)
            out[8 * (j % 4):8 * (j % 4) + 8, TILE * e:TILE * (e + 1)] = chunk[0:8]
            gin[8 * e + j:8 * e + j + 1, :] = chunk[8:9]
            if e == 0:
                small[j:j + 1, :] = chunk[9:10]
    ar_row = small[5:6, :] * (0.5 * ALPHA)
    gout[...] = wcol * ar_row
    ghead[...] = small[4:5, 0:CH] + hdot(jnp.broadcast_to(ar_row, (8, TILE)), wout_f, 1, 1)[0:1]
    gbias[...] = small[0:NOFF, 0:CH]

    for c in pay_c + flag_c + off_c + e_c + x_c + s_c + g_c + c_c + z_c + f_c:
        c.wait_send()


def write_out(*refs):
    n = (len(refs) - 1) // 2
    copies = [pltpu.make_async_copy(refs[i], refs[n + i], refs[-1].at[i]) for i in range(n)]
    for c in copies:
        c.start()
    for c in copies:
        c.wait()


def on_device(emb, wl, wr, win, wout, whead, dbias, offsets, vbins, target):
    def keep(x):
        return pltpu.with_memory_space_constraint(x, pltpu.HBM)

    vm = pl.BlockSpec(memory_space=pltpu.VMEM)
    hbm = pl.BlockSpec(memory_space=pltpu.HBM)
    sd = jax.ShapeDtypeStruct
    dma = pltpu.SemaphoreType.DMA
    out_shape = (
        sd((TILE, TILE), BF16), sd((TILE, TILE), BF16), sd((CH, 512), F32), sd((CH, 512), F32),
        sd((CH, HID), F32), sd((CH, HID), F32), sd((1, CH), F32), sd((NOFF, CH), F32),
    )
    outs = pl.pallas_call(
        kernel,
        out_shape=out_shape,
        in_specs=[hbm] * 7 + [pl.BlockSpec(memory_space=pltpu.SMEM)] + [hbm] * 2,
        out_specs=(vm,) * 8,
        scratch_shapes=[
            pltpu.VMEM((TILE, 512), BF16),
            pltpu.VMEM((CH, 512), BF16),
            pltpu.VMEM((CH, 512), BF16),
            pltpu.VMEM((CH, HID), BF16),
            pltpu.VMEM((CH, HID), BF16),
            pltpu.VMEM((1, CH), F32),
            pltpu.VMEM((NOFF, CH), F32),
            pltpu.VMEM((1, TILE), jnp.int32),
            pltpu.VMEM((TILE, TILE), BF16),
            dma((9,)),
            pltpu.VMEM((HID, TILE, TILE), F32),
            pltpu.VMEM((HID, TILE, TILE), F32),
            pltpu.VMEM((HID, TILE, TILE), F32),
            pltpu.VMEM((HID, TILE), F32),
            pltpu.VMEM((HID, TILE), F32),
            pltpu.VMEM((HID, TILE), F32),
            pltpu.VMEM((HID, TILE), F32),
            pltpu.VMEM((HID, TILE), F32),
            pltpu.VMEM((CH, TILE), BF16),
            pltpu.VMEM((3, CH, TILE), BF16),
            pltpu.VMEM((16, TILE), BF16),
            pltpu.VMEM((3, 16, TILE), BF16),
            pltpu.VMEM((8, TILE), F32),
            pltpu.VMEM((3, 8, TILE), F32),
            pltpu.VMEM((3, TILE, TILE), BF16),
            pltpu.VMEM((2 * CH, TILE), BF16),
            pltpu.VMEM((3, 2 * CH, TILE), BF16),
            pltpu.VMEM((BAND, 16, TILE), F32),
            pltpu.VMEM((3, 16, TILE), F32),
            pltpu.VMEM((8, TILE), F32),
            pltpu.VMEM((GROUPS, 16, TILE), F32),
            pltpu.VMEM((GROUPS - 1, 16, TILE), F32),
            pltpu.VMEM((RING, 16, TILE), BF16),
            pltpu.VMEM((GROUPS * BAND, 16, TILE), BF16),
            pltpu.VMEM((3, CH, TILE), BF16),
            pltpu.VMEM((3, CH, TILE), BF16),
            dma((3,)), dma((3,)), dma((3,)), dma((3,)), dma((3,)), dma((3,)), dma((3,)), dma((3,)), dma((3,)), dma((3,)),
            dma((3,)), dma((3,)), dma((7,)), dma((7,)), dma((15,)), dma((16,)), dma((31,)), dma((32,)), dma((3,)), dma((3,)),
            pltpu.SemaphoreType.REGULAR, pltpu.SemaphoreType.REGULAR,
        ],
        compiler_params=pltpu.CompilerParams(
            collective_id=0, has_side_effects=True, vmem_limit_bytes=48 * 1024 * 1024
        ),
        name="step",
    )(
        keep(emb), keep(wl.T), keep(wr.T), keep(win), keep(wout.T), keep(whead.reshape(1, CH)), keep(dbias.T),
        offsets, keep(vbins.reshape(1, TILE)), keep(target.reshape(TILE, TILE)),
    )
    pred, gemb, gl, gr, gin, gout, ghead, gbias = pl.pallas_call(
        write_out,
        out_shape=out_shape,
        in_specs=[vm] * 8,
        out_specs=(hbm,) * 8,
        scratch_shapes=[dma((8,))],
        compiler_params=pltpu.CompilerParams(vmem_limit_bytes=1024 * 1024),
        name="write_out",
    )(*outs)
    return (
        pred.reshape(1, 1, TILE, TILE), gemb, gl.T, gr.T, gin, gout.T, ghead.reshape(CH), gbias.T,
    )


def solution(mesh):
    return jax.shard_map(
        on_device,
        mesh=mesh,
        in_specs=(
            P("rows", None), P(), P(), P(), P(), P(), P(), P("rows", "band"), P("rows"),
            P("rows", "band", None, None),
        ),
        out_specs=(P("rows", "band", None, None), P("rows", "band"), P(), P(), P(), P(), P(), P()),
        check_vma=False,
    )
```

```python
import functools

import jax
import jax.numpy as jnp
from jax import lax
from jax.experimental import pallas as pl
from jax.experimental.pallas import tpu as pltpu
from jax.sharding import PartitionSpec as P

TILE = 128
NOFF = 4
CH = 32
HID = 128
ROWS = 128
RING = 16
GROUPS = 8
BAND = 4
GROUP_OFFSETS = ((2, 1), (2, 0), (1, 1), (3, 1), (1, 0), (3, 0), (0, 1))
BAND_OFFSETS = ((1, 1), (1, 0), (0, 1))
ALL_OFFSETS = sorted(
    (
        (dy, dx, dh, dc)
        for dy in range(4) for dx in range(2) for dh in range(2) for dc in range(2)
        if dy or dx or dh or dc
    ),
    key=lambda o: (-min(o[0], 4 - o[0]) - (1 if o[1] else 2 * o[2]), -o[3]),
)
MESH = pl.DeviceIdType.MESH
F32 = jnp.float32
BF16 = jnp.bfloat16

C0 = 0.7978845608028654
C1 = C0 * 0.044715
ALPHA = C1 ** (-1.0 / 3.0)
BETA = C0 * ALPHA


def hdot(a, b, ca, cb):
    return lax.dot_general(
        a, b, (((ca,), (cb,)), ((), ())), precision=lax.Precision.HIGHEST, preferred_element_type=F32
    )


def bdot(a, b, ca, cb):
    return lax.dot_general(a, b, (((ca,), (cb,)), ((), ())), preferred_element_type=F32)


def halves(x):
    hi = x.astype(BF16)
    return hi, (x - hi.astype(F32)).astype(BF16)


def kernel(
    emb_h, wl_h, wr_h, win_h, wout_h, whead_h, dbias_h, off_h, vbins_h, tgt_h,
    pred, gemb, gl, gr, gin, gout, ghead, gbias,
    emb, wl, wr, win, wout, whead, dbias, vbins, tgt, load_s,
    lhs, spread, act, slope, b_s, v_s, gr_s, gc_s, ar_s,
    pay, pay_in, flag_out, flag_in, off_out, off_in, e_in,
    x_out, x_in, s_out, s_in, small,
    rs_out, rs_in, zbuf, fin, c_out, c_in,
    pay_ss, pay_rs, flag_ss, flag_rs, off_ss, off_rs, e_ss, e_rs, x_ss, x_rs, s_ss, s_rs, g_ss, g_rs, z_ss, z_rs, f_ss, f_rs, c_ss, c_rs, here, there,
):
    r = lax.axis_index("rows")
    b = lax.axis_index("band")
    z = lax.rem(r, RING)
    base = r - z
    g = lax.div(r, RING)
    gy, gx = lax.div(g, 2), lax.rem(g, 2)
    bh, bc = lax.div(b, 2), lax.rem(b, 2)

    def row_at(d):
        return lax.rem(r + (d + ROWS), ROWS)

    def ring_at(d):
        return base + lax.rem(z + d, RING)

    def group_index(dy, dx):
        return lax.rem(gy + dy, 4) * 2 + lax.rem(gx + dx, 2)

    def group_at(dy, dx):
        return group_index(dy, dx) * RING + z

    def band_at(dh, dc):
        return lax.rem(bh + dh, 2) * 2 + lax.rem(bc + dc, 2)

    def signal(sem, dev):
        pl.semaphore_signal(sem, inc=1, device_id=dev, device_id_type=MESH)

    def remote(src, dst, ss, rs, dev):
        return pltpu.make_async_remote_copy(
            src_ref=src, dst_ref=dst, send_sem=ss, recv_sem=rs, device_id=dev, device_id_type=MESH
        )

    barrier = pltpu.get_barrier_semaphore()
    near = [(row_at(d), b) for d in (-3, 3, -2, 2, -1, 1)]
    for dev in near:
        signal(barrier, dev)
    loads = [
        pltpu.make_async_copy(src, dst, load_s.at[n])
        for n, (src, dst) in enumerate(
            [
                (wr_h, wr), (emb_h, emb), (wl_h, wl), (vbins_h, vbins), (win_h, win), (wout_h, wout),
                (whead_h, whead), (dbias_h, dbias), (tgt_h, tgt),
            ]
        )
    ]
    for c in loads:
        c.start()
    rest = [(group_at(dy, dx), b) for dy, dx in GROUP_OFFSETS]
    rest += [(r, band_at(dh, dc)) for dh, dc in BAND_OFFSETS]
    rest += [(ring_at(d), b) for d in (2, 14, 1, 15)]
    for dev in rest:
        signal(barrier, dev)

    for c in loads[:4]:
        c.wait()
    right_b = bdot(wr[...], emb[...], 1, 1).astype(BF16)
    right = right_b.astype(F32)
    flags = vbins[...].astype(F32)
    pay[...] = right_b
    flag_out[...] = jnp.broadcast_to(flags, (16, TILE)).astype(BF16)

    pl.semaphore_wait(barrier, len(near) + len(rest))
    pay_c = [
        remote(pay, pay_in.at[d - 1], pay_ss.at[d - 1], pay_rs.at[d - 1], (row_at(-d), b)) for d in (3, 2, 1)
    ]
    for c in pay_c:
        c.start()
    flag_c = [
        remote(flag_out, flag_in.at[d - 1], flag_ss.at[d - 1], flag_rs.at[d - 1], (row_at(-d), b)) for d in (3, 2, 1)
    ]
    offset = off_h[0, 0]
    off_out[...] = jnp.full((8, TILE), offset.astype(F32), F32)
    off_c = [
        remote(off_out, off_in.at[n], off_ss.at[n], off_rs.at[n], (r, band_at(dh, dc)))
        for n, (dh, dc) in enumerate(BAND_OFFSETS)
    ]
    for c in flag_c + off_c:
        c.start()
    for dy, dx in GROUP_OFFSETS:
        signal(here, (group_at(dy, dx), b))
    for d in (2, 14):
        signal(here, (ring_at(d), b))

    share = pl.ds(pl.multiple_of(b * TILE, TILE), TILE)
    left = bdot(wl[...], emb[...], 1, 1).astype(BF16).astype(F32)
    ltf = jnp.transpose(left)
    for c in loads[4:]:
        c.wait()
    wh = whead[...]
    eye = lax.broadcasted_iota(jnp.int32, (CH, CH), 0) == lax.broadcasted_iota(jnp.int32, (CH, CH), 1)
    wcol = jnp.sum(jnp.where(eye, wh, 0.0), axis=1, keepdims=True)
    wout_f = wout[...].astype(F32)
    win_f = win[...].astype(F32)
    win_t = jnp.transpose(win_f)
    v_row = jnp.sum(wout_f * wcol, axis=0, keepdims=True)
    v_s[...] = jnp.transpose(jnp.broadcast_to(v_row, (TILE, HID)))
    wcol_lin = wcol + 0.5 * jnp.sum(win_f * v_row, axis=1, keepdims=True)
    wrow_lin = jnp.sum(jnp.where(eye, wcol_lin, 0.0), axis=0, keepdims=True)
    row_logit = jnp.sum(ltf * wrow_lin, axis=1, keepdims=True)
    hot = [jnp.where(offset == j, 1.0, 0.0).astype(F32) for j in range(NOFF)]
    bias_row = sum(dbias[j:j + 1, :] * hot[j] for j in range(NOFF))
    bias_col = jnp.sum(jnp.where(eye, bias_row, 0.0), axis=1, keepdims=True)
    b_s[...] = hdot(win_t, jnp.broadcast_to(bias_col, (CH, TILE)), 1, 0) * (1.0 / ALPHA)
    row_flags = jnp.sum(
        jnp.where(
            lax.broadcasted_iota(jnp.int32, (TILE, TILE), 0) == lax.broadcasted_iota(jnp.int32, (TILE, TILE), 1),
            flags, 0.0,
        ),
        axis=1, keepdims=True,
    )
    tgt_f = tgt[...].astype(F32)
    a = bdot(win_t.astype(BF16), left.astype(BF16), 1, 0) * (1.0 / ALPHA)
    a_hi = a.astype(BF16).astype(F32)
    a_lo = a - a_hi
    ones_16 = jnp.ones((16, TILE), F32)
    for m in range(4):
        parts = []
        for i in range(4 * m, 4 * m + 4):
            parts += [a_hi[8 * i:8 * i + 8], a_lo[8 * i:8 * i + 8], ones_16]
        turned = jnp.transpose(jnp.concatenate(parts, axis=0)).astype(BF16)
        for i in range(4):
            lhs[4 * m + i] = turned[:, 32 * i:32 * i + 32]
    spread[...] = jnp.where(
        lax.rem(lax.broadcasted_iota(jnp.int32, (16, 8 * TILE), 0), 8)
        == lax.div(lax.broadcasted_iota(jnp.int32, (16, 8 * TILE), 1), TILE),
        1.0, 0.0,
    ).astype(BF16)
    for j in range(GROUPS):
        rs_out[j, 8:16] = jnp.zeros((8, TILE), F32)

    pl.semaphore_wait(here, len(GROUP_OFFSETS) + 2)
    for d in (4, 12):
        signal(there, (ring_at(d), b))

    weight = [hot[0]] + [hot[d] * jnp.where(r + d < ROWS, 1.0, 0.0).astype(F32) for d in (1, 2, 3)]
    r_sel = right * weight[0]
    for c in pay_c:
        c.wait_recv()
    for d in (1, 2, 3):
        r_sel = r_sel + pay_in[d - 1].astype(F32) * weight[d]

    e_c = [
        remote(emb.at[:, share], e_in.at[d - 1], e_ss.at[d - 1], e_rs.at[d - 1], (row_at(-d), b)) for d in (3, 2, 1)
    ]
    for c in e_c:
        c.start()

    r_b = r_sel + bias_col
    b_s[...] += bdot(win_t.astype(BF16), r_sel.astype(BF16), 1, 0) * (1.0 / ALPHA)
    col_logit = jnp.sum(r_b * wcol_lin, axis=0, keepdims=True)
    p_hi, p_lo = halves(jnp.concatenate([left, r_b], axis=1))
    p_3 = jnp.concatenate([p_hi, p_hi, p_lo], axis=1)

    def first(i, total):
        b8 = b_s[pl.ds(pl.multiple_of(8 * i, 8), 8), :]
        b_hi = b8.astype(BF16).astype(F32)
        b_16 = jnp.concatenate([b_hi, b8 - b_hi], axis=0).astype(BF16)
        mask = spread[...]
        rhs = jnp.concatenate([mask, jnp.concatenate([b_16] * 8, axis=1) * mask], axis=0)
        y_8 = bdot(lhs[i], rhs, 1, 0)
        for j in range(8):
            k = 8 * i + j
            y = y_8[:, TILE * j:TILE * (j + 1)]
            w = y * y + BETA
            t = jnp.tanh(y * w)
            yt = y * t
            act[k] = yt
            slope[k] = t + (y - t * yt) * (3.0 * w - 2.0 * BETA)
            total = total + yt * v_s[pl.ds(k, 1), :]
        return total

    total = lax.fori_loop(0, HID // 8, first, jnp.zeros((TILE, TILE), F32), unroll=4)
    logits = total * (0.5 * ALPHA) + (row_logit + col_logit)
    pred[...] = logits.astype(BF16)
    f_sel = flags * weight[0]
    for c in flag_c:
        c.wait_recv()
    for d in (1, 2, 3):
        f_sel = f_sel + flag_in[d - 1, 0:1].astype(F32) * weight[d]
    res = (row_flags * f_sel) * (logits - tgt_f) * (1.0 / (NOFF * TILE))
    ones = jnp.ones((8, TILE), BF16)

    parts = []
    for k in range(HID):
        h = slope[k] * res
        gc_s[k:k + 1, :] = jnp.sum(h, axis=0, keepdims=True)
        ar_s[k:k + 1, :] = jnp.sum(act[k] * res, axis=0, keepdims=True)
        parts.append(h.astype(BF16))
    over_q = bdot(ones, jnp.concatenate(parts, axis=0), 1, 1)
    for k in range(HID):
        gr_s[k:k + 1, :] = over_q[0:1, TILE * k:TILE * (k + 1)]

    half_v = v_s[...] * 0.5
    res_hi, res_lo = halves(res)
    rr = bdot(jnp.ones((8, 2 * TILE), BF16), jnp.concatenate([res_hi, res_lo], axis=1), 1, 1)
    rc = jnp.broadcast_to(jnp.sum(res, axis=0, keepdims=True), (8, TILE))
    r_both = jnp.concatenate([rr, rc], axis=1)
    g_both = jnp.concatenate([(gr_s[...] + rr[0:1]) * half_v, (gc_s[...] + rc[0:1]) * half_v], axis=1)
    g_hi, g_lo = halves(g_both)
    sums = wcol * r_both[0:1] + bdot(
        jnp.concatenate([win[...], win[...]], axis=1), jnp.concatenate([g_hi, g_lo], axis=0), 1, 0
    )
    sums_b = sums.astype(BF16)

    x_out[0:CH] = sums_b[:, :TILE]
    x_out[CH:2 * CH] = sums_b[:, TILE:]
    x_c, s_c = [], []
    for n, (dh, dc) in enumerate(BAND_OFFSETS):
        dev = (r, band_at(dh, dc))
        x_c.append(remote(x_out, x_in.at[n], x_ss.at[n], x_rs.at[n], dev))
        s_c.append(remote(s_out.at[band_at(dh, dc)], s_in.at[n], s_ss.at[n], s_rs.at[n], dev))
    for c in x_c:
        c.start()
    r_hi, r_lo = halves(r_both)
    gin_part = bdot(p_3, jnp.concatenate([g_hi, g_lo, g_hi], axis=1), 1, 1)
    head = bdot(jnp.concatenate([r_hi, r_lo, r_hi], axis=1), p_3, 1, 1)
    ones_2 = jnp.ones((8, 2 * TILE), BF16)
    bias = bdot(ones_2, jnp.concatenate(halves(sums[:, :TILE]), axis=1), 1, 1)
    h_hi, h_lo = halves(head)
    ar = bdot(ones_2, jnp.concatenate(halves(ar_s[...]), axis=1), 1, 1) + bdot(
        jnp.concatenate([h_hi, h_lo], axis=1), jnp.concatenate([win[...], win[...]], axis=0), 1, 0
    ) * (1.0 / ALPHA)
    row_id = lax.broadcasted_iota(jnp.int32, (8, TILE), 0)
    small[...] = jnp.where(row_id == 5, ar, 0.0)
    for j in range(NOFF):
        small[j:j + 1, 0:CH] = bias[0:1] * hot[j]
    small[4:5, 0:CH] = head[0:1]
    extra = small[...]
    for e in range(BAND):
        s_out[e, 0:8] = gin_part[8 * e:8 * e + 8]
        s_out[e, 8:16] = extra
    for c in s_c:
        c.start()
    for c in e_c + off_c + x_c:
        c.wait_recv()
    own = sums_b.astype(F32)
    row_tot = own[:, :TILE]
    cols = [own[:, TILE:] * hot[j] for j in range(NOFF)]
    for n in range(BAND - 1):
        got = x_in[n].astype(F32)
        row_tot = row_tot + got[:CH]
        its_offset = off_in[n, 0:1, :]
        for j in range(NOFF):
            cols[j] = cols[j] + jnp.where(its_offset == j, got[CH:], 0.0)
    row_b = row_tot.astype(BF16)
    cols_b = [c.astype(BF16) for c in cols]
    near_part = bdot(jnp.concatenate([row_b, cols_b[0]], axis=0), emb[:, share], 1, 0)
    part_l = near_part[:CH]
    part_r = near_part[CH:] + bdot(
        jnp.concatenate(cols_b[1:], axis=1), jnp.concatenate([e_in[d] for d in range(3)], axis=0), 1, 0
    )
    for j in range(4):
        rs_out[j, 0:8] = part_l[8 * j:8 * j + 8]
        rs_out[4 + j, 0:8] = part_r[8 * j:8 * j + 8]
    mine = s_out[b]
    for c in s_c:
        c.wait_recv()
    for n in range(BAND - 1):
        mine = mine + s_in[n]
    for j in range(GROUPS):
        rs_out[j, 8:9] = mine[j:j + 1]
        rs_out[j, 9:10] = mine[8 + j:9 + j]

    g_c = [
        remote(
            rs_out.at[group_index(dy, dx)], rs_in.at[n], g_ss.at[n], g_rs.at[n], (group_at(dy, dx), b)
        )
        for n, (dy, dx) in enumerate(GROUP_OFFSETS)
    ]
    for c in g_c:
        c.start()
    for d in (1, 2, 3):
        c_out[d - 1] = cols_b[d]
    c_c = [
        remote(c_out.at[d - 1], c_in.at[d - 1], c_ss.at[d - 1], c_rs.at[d - 1], (row_at(d), b)) for d in (3, 2, 1)
    ]
    for c in c_c:
        c.start()
    mine = rs_out[g]
    for c in g_c:
        c.wait_recv()
    for d in range(GROUPS - 1):
        mine = mine + rs_in[d]
    zbuf[z] = mine.astype(BF16)

    pl.semaphore_wait(there, 2)
    z_c = [
        remote(
            zbuf.at[z], zbuf.at[z], z_ss.at[d - 1], z_rs.at[z], (ring_at(d), b)
        )
        for d in (8, 7, 9, 6, 10, 5, 11, 4, 12, 3, 13, 2, 14, 1, 15)
    ]
    for c in z_c:
        c.start()

    for c in c_c:
        c.wait_recv()
    col_tot = cols[0]
    for d in (1, 2, 3):
        col_tot = col_tot + c_in[d - 1].astype(F32)
    both_t = jnp.transpose(jnp.concatenate([row_tot, col_tot], axis=0)).astype(BF16)
    w_both = jnp.concatenate([wl[:, share], wr[:, share]], axis=0)
    gemb[...] = bdot(both_t, w_both, 1, 0).astype(BF16)

    for d in range(1, RING):
        at_z = lax.rem(z + d, RING)
        remote(zbuf.at[z], zbuf.at[at_z], z_ss.at[d - 1], z_rs.at[at_z], (ring_at(d), b)).wait_recv()
    whole = zbuf[0].astype(F32)
    for d in range(1, RING):
        whole = whole + zbuf[d].astype(F32)
    me = g * BAND + b
    fin[me] = whole.astype(BF16)

    f_c = [
        remote(fin.at[me], fin.at[me], f_ss.at[n], f_rs.at[me], (group_at(dy, dx), band_at(dh, dc)))
        for n, (dy, dx, dh, dc) in enumerate(ALL_OFFSETS)
    ]
    for c in f_c:
        c.start()
    for n, (dy, dx, dh, dc) in reversed(list(enumerate(ALL_OFFSETS))):
        src = group_index(dy, dx) * BAND + band_at(dh, dc)
        remote(
            fin.at[me], fin.at[src], f_ss.at[n], f_rs.at[src], (group_at(dy, dx), band_at(dh, dc))
        ).wait_recv()
    for j in range(GROUPS):
        out = gl if j < 4 else gr
        for e in range(BAND):
            chunk = fin[j * BAND + e].astype(F32)
            out[8 * (j % 4):8 * (j % 4) + 8, TILE * e:TILE * (e + 1)] = chunk[0:8]
            gin[8 * e + j:8 * e + j + 1, :] = chunk[8:9]
            if e == 0:
                small[j:j + 1, :] = chunk[9:10]
    ar_row = small[5:6, :] * (0.5 * ALPHA)
    gout[...] = wcol * ar_row
    ghead[...] = small[4:5, 0:CH] + bdot(
        jnp.concatenate(halves(jnp.broadcast_to(ar_row, (8, TILE))), axis=1),
        jnp.concatenate([wout[...], wout[...]], axis=1), 1, 1,
    )[0:1]
    gbias[...] = small[0:NOFF, 0:CH]

    for c in pay_c + flag_c + off_c + e_c + x_c + s_c + g_c + c_c + z_c + f_c:
        c.wait_send()


def write_out(*refs):
    n = (len(refs) - 1) // 2
    copies = [pltpu.make_async_copy(refs[i], refs[n + i], refs[-1].at[i]) for i in range(n)]
    for c in copies:
        c.start()
    for c in copies:
        c.wait()


def on_device(emb, wl, wr, win, wout, whead, dbias, offsets, vbins, target):
    def keep(x):
        return pltpu.with_memory_space_constraint(x, pltpu.HBM)

    vm = pl.BlockSpec(memory_space=pltpu.VMEM)
    hbm = pl.BlockSpec(memory_space=pltpu.HBM)
    sd = jax.ShapeDtypeStruct
    dma = pltpu.SemaphoreType.DMA
    out_shape = (
        sd((TILE, TILE), BF16), sd((TILE, TILE), BF16), sd((CH, 512), F32), sd((CH, 512), F32),
        sd((CH, HID), F32), sd((CH, HID), F32), sd((1, CH), F32), sd((NOFF, CH), F32),
    )
    outs = pl.pallas_call(
        kernel,
        out_shape=out_shape,
        in_specs=[hbm] * 7 + [pl.BlockSpec(memory_space=pltpu.SMEM)] + [hbm] * 2,
        out_specs=(vm,) * 8,
        scratch_shapes=[
            pltpu.VMEM((TILE, 512), BF16),
            pltpu.VMEM((CH, 512), BF16),
            pltpu.VMEM((CH, 512), BF16),
            pltpu.VMEM((CH, HID), BF16),
            pltpu.VMEM((CH, HID), BF16),
            pltpu.VMEM((1, CH), F32),
            pltpu.VMEM((NOFF, CH), F32),
            pltpu.VMEM((1, TILE), jnp.int32),
            pltpu.VMEM((TILE, TILE), BF16),
            dma((9,)),
            pltpu.VMEM((HID // 8, TILE, 32), BF16),
            pltpu.VMEM((16, 8 * TILE), BF16),
            pltpu.VMEM((HID, TILE, TILE), F32),
            pltpu.VMEM((HID, TILE, TILE), F32),
            pltpu.VMEM((HID, TILE), F32),
            pltpu.VMEM((HID, TILE), F32),
            pltpu.VMEM((HID, TILE), F32),
            pltpu.VMEM((HID, TILE), F32),
            pltpu.VMEM((HID, TILE), F32),
            pltpu.VMEM((CH, TILE), BF16),
            pltpu.VMEM((3, CH, TILE), BF16),
            pltpu.VMEM((16, TILE), BF16),
            pltpu.VMEM((3, 16, TILE), BF16),
            pltpu.VMEM((8, TILE), F32),
            pltpu.VMEM((3, 8, TILE), F32),
            pltpu.VMEM((3, TILE, TILE), BF16),
            pltpu.VMEM((2 * CH, TILE), BF16),
            pltpu.VMEM((3, 2 * CH, TILE), BF16),
            pltpu.VMEM((BAND, 16, TILE), F32),
            pltpu.VMEM((3, 16, TILE), F32),
            pltpu.VMEM((8, TILE), F32),
            pltpu.VMEM((GROUPS, 16, TILE), F32),
            pltpu.VMEM((GROUPS - 1, 16, TILE), F32),
            pltpu.VMEM((RING, 16, TILE), BF16),
            pltpu.VMEM((GROUPS * BAND, 16, TILE), BF16),
            pltpu.VMEM((3, CH, TILE), BF16),
            pltpu.VMEM((3, CH, TILE), BF16),
            dma((3,)), dma((3,)), dma((3,)), dma((3,)), dma((3,)), dma((3,)), dma((3,)), dma((3,)), dma((3,)), dma((3,)),
            dma((3,)), dma((3,)), dma((7,)), dma((7,)), dma((15,)), dma((16,)), dma((31,)), dma((32,)), dma((3,)), dma((3,)),
            pltpu.SemaphoreType.REGULAR, pltpu.SemaphoreType.REGULAR,
        ],
        compiler_params=pltpu.CompilerParams(
            collective_id=0, has_side_effects=True, vmem_limit_bytes=48 * 1024 * 1024
        ),
        name="step",
    )(
        keep(emb), keep(wl.T), keep(wr.T), keep(win), keep(wout.T), keep(whead.reshape(1, CH)), keep(dbias.T),
        offsets, keep(vbins.reshape(1, TILE)), keep(target.reshape(TILE, TILE)),
    )
    pred, gemb, gl, gr, gin, gout, ghead, gbias = pl.pallas_call(
        write_out,
        out_shape=out_shape,
        in_specs=[vm] * 8,
        out_specs=(hbm,) * 8,
        scratch_shapes=[dma((8,))],
        compiler_params=pltpu.CompilerParams(vmem_limit_bytes=1024 * 1024),
        name="write_out",
    )(*outs)
    return (
        pred.reshape(1, 1, TILE, TILE), gemb, gl.T, gr.T, gin, gout.T, ghead.reshape(CH), gbias.T,
    )


def solution(mesh):
    return jax.shard_map(
        on_device,
        mesh=mesh,
        in_specs=(
            P("rows", None), P(), P(), P(), P(), P(), P(), P("rows", "band"), P("rows"),
            P("rows", "band", None, None),
        ),
        out_specs=(P("rows", "band", None, None), P("rows", "band"), P(), P(), P(), P(), P(), P()),
        check_vma=False,
    )
```

```python
import functools

import jax
import jax.numpy as jnp
from jax import lax
from jax.experimental import pallas as pl
from jax.experimental.pallas import tpu as pltpu
from jax.sharding import PartitionSpec as P

TILE = 128
NOFF = 4
CH = 32
HID = 128
ROWS = 128
RING = 16
GROUPS = 8
BAND = 4
GROUP_OFFSETS = ((2, 1), (2, 0), (1, 1), (3, 1), (1, 0), (3, 0), (0, 1))
BAND_OFFSETS = ((1, 1), (1, 0), (0, 1))
ALL_OFFSETS = sorted(
    (
        (dy, dx, dh, dc)
        for dy in range(4) for dx in range(2) for dh in range(2) for dc in range(2)
        if dy or dx or dh or dc
    ),
    key=lambda o: (-min(o[0], 4 - o[0]) - (1 if o[1] else 2 * o[2]), -o[3]),
)
MESH = pl.DeviceIdType.MESH
F32 = jnp.float32
BF16 = jnp.bfloat16

C0 = 0.7978845608028654
C1 = C0 * 0.044715
ALPHA = C1 ** (-1.0 / 3.0)
BETA = C0 * ALPHA


def hdot(a, b, ca, cb):
    return lax.dot_general(
        a, b, (((ca,), (cb,)), ((), ())), precision=lax.Precision.HIGHEST, preferred_element_type=F32
    )


def bdot(a, b, ca, cb):
    return lax.dot_general(a, b, (((ca,), (cb,)), ((), ())), preferred_element_type=F32)


def halves(x):
    hi = x.astype(BF16)
    return hi, (x - hi.astype(F32)).astype(BF16)


def kernel(
    emb_h, wl_h, wr_h, win_h, wout_h, whead_h, dbias_h, off_h, vbins_h, tgt_h,
    pred, gemb, gl, gr, gin, gout, ghead, gbias,
    emb, wl, wr, win, wout, whead, dbias, vbins, tgt, load_s,
    lhs, spread, act, slope, b_s, v_s, gr_s, gc_s, ar_s,
    pay, pay_in, flag_out, flag_in, off_out, off_in, e_in,
    x_out, x_in, s_out, s_in, small, tail,
    rs_out, rs_in, zbuf, fin, c_out, c_in,
    pay_ss, pay_rs, flag_ss, flag_rs, off_ss, off_rs, e_ss, e_rs, x_ss, x_rs, s_ss, s_rs, g_ss, g_rs, z_ss, z_rs, f_ss, f_rs, c_ss, c_rs, here, there,
):
    r = lax.axis_index("rows")
    b = lax.axis_index("band")
    z = lax.rem(r, RING)
    base = r - z
    g = lax.div(r, RING)
    gy, gx = lax.div(g, 2), lax.rem(g, 2)
    bh, bc = lax.div(b, 2), lax.rem(b, 2)

    def row_at(d):
        return lax.rem(r + (d + ROWS), ROWS)

    def ring_at(d):
        return base + lax.rem(z + d, RING)

    def group_index(dy, dx):
        return lax.rem(gy + dy, 4) * 2 + lax.rem(gx + dx, 2)

    def group_at(dy, dx):
        return group_index(dy, dx) * RING + z

    def band_at(dh, dc):
        return lax.rem(bh + dh, 2) * 2 + lax.rem(bc + dc, 2)

    def signal(sem, dev):
        pl.semaphore_signal(sem, inc=1, device_id=dev, device_id_type=MESH)

    def remote(src, dst, ss, rs, dev):
        return pltpu.make_async_remote_copy(
            src_ref=src, dst_ref=dst, send_sem=ss, recv_sem=rs, device_id=dev, device_id_type=MESH
        )

    barrier = pltpu.get_barrier_semaphore()
    near = [(row_at(d), b) for d in (-3, 3, -2, 2, -1, 1)]
    for dev in near:
        signal(barrier, dev)
    loads = [
        pltpu.make_async_copy(src, dst, load_s.at[n])
        for n, (src, dst) in enumerate(
            [
                (wr_h, wr), (emb_h, emb), (wl_h, wl), (vbins_h, vbins), (win_h, win), (wout_h, wout),
                (whead_h, whead), (dbias_h, dbias), (tgt_h, tgt),
            ]
        )
    ]
    for c in loads:
        c.start()
    rest = [(group_at(dy, dx), b) for dy, dx in GROUP_OFFSETS]
    rest += [(r, band_at(dh, dc)) for dh, dc in BAND_OFFSETS]
    rest += [(ring_at(d), b) for d in (2, 14, 1, 15)]
    for dev in rest:
        signal(barrier, dev)

    for c in loads[:4]:
        c.wait()
    right_b = bdot(wr[...], emb[...], 1, 1).astype(BF16)
    right = right_b.astype(F32)
    flags = vbins[...].astype(F32)
    pay[...] = right_b
    flag_out[...] = jnp.broadcast_to(flags, (16, TILE)).astype(BF16)

    pl.semaphore_wait(barrier, len(near) + len(rest))
    pay_c = [
        remote(pay, pay_in.at[d - 1], pay_ss.at[d - 1], pay_rs.at[d - 1], (row_at(-d), b)) for d in (3, 2, 1)
    ]
    for c in pay_c:
        c.start()
    flag_c = [
        remote(flag_out, flag_in.at[d - 1], flag_ss.at[d - 1], flag_rs.at[d - 1], (row_at(-d), b)) for d in (3, 2, 1)
    ]
    offset = off_h[0, 0]
    off_out[...] = jnp.full((8, TILE), offset.astype(F32), F32)
    off_c = [
        remote(off_out, off_in.at[n], off_ss.at[n], off_rs.at[n], (r, band_at(dh, dc)))
        for n, (dh, dc) in enumerate(BAND_OFFSETS)
    ]
    for c in flag_c + off_c:
        c.start()
    for dy, dx in GROUP_OFFSETS:
        signal(here, (group_at(dy, dx), b))
    for d in (2, 14):
        signal(here, (ring_at(d), b))

    share = pl.ds(pl.multiple_of(b * TILE, TILE), TILE)
    left = bdot(wl[...], emb[...], 1, 1).astype(BF16).astype(F32)
    ltf = jnp.transpose(left)
    for c in loads[4:]:
        c.wait()
    wh = whead[...]
    eye = lax.broadcasted_iota(jnp.int32, (CH, CH), 0) == lax.broadcasted_iota(jnp.int32, (CH, CH), 1)
    wcol = jnp.sum(jnp.where(eye, wh, 0.0), axis=1, keepdims=True)
    wout_f = wout[...].astype(F32)
    win_f = win[...].astype(F32)
    win_t = jnp.transpose(win_f)
    v_row = jnp.sum(wout_f * wcol, axis=0, keepdims=True)
    v_s[...] = jnp.transpose(jnp.broadcast_to(v_row, (TILE, HID)))
    wcol_lin = wcol + 0.5 * jnp.sum(win_f * v_row, axis=1, keepdims=True)
    wrow_lin = jnp.sum(jnp.where(eye, wcol_lin, 0.0), axis=0, keepdims=True)
    row_logit = jnp.sum(ltf * wrow_lin, axis=1, keepdims=True)
    hot = [jnp.where(offset == j, 1.0, 0.0).astype(F32) for j in range(NOFF)]
    bias_row = sum(dbias[j:j + 1, :] * hot[j] for j in range(NOFF))
    bias_col = jnp.sum(jnp.where(eye, bias_row, 0.0), axis=1, keepdims=True)
    b_s[...] = hdot(win_t, jnp.broadcast_to(bias_col, (CH, TILE)), 1, 0) * (1.0 / ALPHA)
    row_flags = jnp.sum(
        jnp.where(
            lax.broadcasted_iota(jnp.int32, (TILE, TILE), 0) == lax.broadcasted_iota(jnp.int32, (TILE, TILE), 1),
            flags, 0.0,
        ),
        axis=1, keepdims=True,
    )
    tgt_f = tgt[...].astype(F32)
    a = bdot(win_t.astype(BF16), left.astype(BF16), 1, 0) * (1.0 / ALPHA)
    a_hi = a.astype(BF16).astype(F32)
    a_lo = a - a_hi
    ones_16 = jnp.ones((16, TILE), F32)
    for m in range(4):
        parts = []
        for i in range(4 * m, 4 * m + 4):
            parts += [a_hi[8 * i:8 * i + 8], a_lo[8 * i:8 * i + 8], ones_16]
        turned = jnp.transpose(jnp.concatenate(parts, axis=0)).astype(BF16)
        for i in range(4):
            lhs[4 * m + i] = turned[:, 32 * i:32 * i + 32]
    spread[...] = jnp.where(
        lax.rem(lax.broadcasted_iota(jnp.int32, (16, 8 * TILE), 0), 8)
        == lax.div(lax.broadcasted_iota(jnp.int32, (16, 8 * TILE), 1), TILE),
        1.0, 0.0,
    ).astype(BF16)
    tail[...] = jnp.zeros_like(tail)

    pl.semaphore_wait(here, len(GROUP_OFFSETS) + 2)
    for d in (4, 12):
        signal(there, (ring_at(d), b))

    weight = [hot[0]] + [hot[d] * jnp.where(r + d < ROWS, 1.0, 0.0).astype(F32) for d in (1, 2, 3)]
    r_sel = right * weight[0]
    for c in pay_c:
        c.wait_recv()
    for d in (1, 2, 3):
        r_sel = r_sel + pay_in[d - 1].astype(F32) * weight[d]

    e_c = [
        remote(emb.at[:, share], e_in.at[d - 1], e_ss.at[d - 1], e_rs.at[d - 1], (row_at(-d), b)) for d in (3, 2, 1)
    ]
    for c in e_c:
        c.start()

    r_b = r_sel + bias_col
    b_s[...] += bdot(win_t.astype(BF16), r_sel.astype(BF16), 1, 0) * (1.0 / ALPHA)
    col_logit = jnp.sum(r_b * wcol_lin, axis=0, keepdims=True)
    p_hi, p_lo = halves(jnp.concatenate([left, r_b], axis=1))
    p_3 = jnp.concatenate([p_hi, p_hi, p_lo], axis=1)

    def first(i, total):
        b8 = b_s[pl.ds(pl.multiple_of(8 * i, 8), 8), :]
        b_hi = b8.astype(BF16).astype(F32)
        b_16 = jnp.concatenate([b_hi, b8 - b_hi], axis=0).astype(BF16)
        mask = spread[...]
        rhs = jnp.concatenate([mask, jnp.concatenate([b_16] * 8, axis=1) * mask], axis=0)
        y_8 = bdot(lhs[i], rhs, 1, 0)
        for j in range(8):
            k = 8 * i + j
            y = y_8[:, TILE * j:TILE * (j + 1)]
            w = y * y + BETA
            t = jnp.tanh(y * w)
            yt = y * t
            act[k] = yt
            slope[k] = t + (y - t * yt) * (3.0 * w - 2.0 * BETA)
            total = total + yt * v_s[pl.ds(k, 1), :]
        return total

    total = lax.fori_loop(0, HID // 8, first, jnp.zeros((TILE, TILE), F32), unroll=4)
    logits = total * (0.5 * ALPHA) + (row_logit + col_logit)
    pred[...] = logits.astype(BF16)
    f_sel = flags * weight[0]
    for c in flag_c:
        c.wait_recv()
    for d in (1, 2, 3):
        f_sel = f_sel + flag_in[d - 1].astype(F32)[0:1] * weight[d]
    res = (row_flags * f_sel) * (logits - tgt_f) * (1.0 / (NOFF * TILE))
    ones = jnp.ones((8, TILE), BF16)

    parts = []
    for k in range(HID):
        h = slope[k] * res
        gc_s[k:k + 1, :] = jnp.sum(h, axis=0, keepdims=True)
        ar_s[k:k + 1, :] = jnp.sum(act[k] * res, axis=0, keepdims=True)
        parts.append(h.astype(BF16))
    over_q = bdot(ones, jnp.concatenate(parts, axis=0), 1, 1)
    for k in range(HID):
        gr_s[k:k + 1, :] = over_q[0:1, TILE * k:TILE * (k + 1)]

    half_v = v_s[...] * 0.5
    res_hi, res_lo = halves(res)
    rr = bdot(jnp.ones((8, 2 * TILE), BF16), jnp.concatenate([res_hi, res_lo], axis=1), 1, 1)
    rc = jnp.broadcast_to(jnp.sum(res, axis=0, keepdims=True), (8, TILE))
    r_both = jnp.concatenate([rr, rc], axis=1)
    g_both = jnp.concatenate([(gr_s[...] + rr[0:1]) * half_v, (gc_s[...] + rc[0:1]) * half_v], axis=1)
    g_hi, g_lo = halves(g_both)
    sums = wcol * r_both[0:1] + bdot(
        jnp.concatenate([win[...], win[...]], axis=1), jnp.concatenate([g_hi, g_lo], axis=0), 1, 0
    )
    sums_b = sums.astype(BF16)

    x_out[0:CH] = sums_b[:, :TILE]
    x_out[CH:2 * CH] = sums_b[:, TILE:]
    x_c, s_c = [], []
    for n, (dh, dc) in enumerate(BAND_OFFSETS):
        dev = (r, band_at(dh, dc))
        x_c.append(remote(x_out, x_in.at[n], x_ss.at[n], x_rs.at[n], dev))
        s_c.append(remote(s_out.at[band_at(dh, dc)], s_in.at[n], s_ss.at[n], s_rs.at[n], dev))
    for c in x_c:
        c.start()
    r_hi, r_lo = halves(r_both)
    gin_part = bdot(p_3, jnp.concatenate([g_hi, g_lo, g_hi], axis=1), 1, 1)
    head = bdot(jnp.concatenate([r_hi, r_lo, r_hi], axis=1), p_3, 1, 1)
    ones_2 = jnp.ones((8, 2 * TILE), BF16)
    bias = bdot(ones_2, jnp.concatenate(halves(sums[:, :TILE]), axis=1), 1, 1)
    h_hi, h_lo = halves(head)
    ar = bdot(ones_2, jnp.concatenate(halves(ar_s[...]), axis=1), 1, 1) + bdot(
        jnp.concatenate([h_hi, h_lo], axis=1), jnp.concatenate([win[...], win[...]], axis=0), 1, 0
    ) * (1.0 / ALPHA)
    row_id = lax.broadcasted_iota(jnp.int32, (8, TILE), 0)
    small[...] = jnp.where(row_id == 5, ar, 0.0)
    for j in range(NOFF):
        small[j:j + 1, 0:CH] = bias[0:1] * hot[j]
    small[4:5, 0:CH] = head[0:1]
    extra = small[...]
    for e in range(BAND):
        s_out[e, 0:8] = gin_part[8 * e:8 * e + 8]
        s_out[e, 8:16] = extra
    for c in s_c:
        c.start()
    for c in e_c + off_c + x_c:
        c.wait_recv()
    own = sums_b.astype(F32)
    row_tot = own[:, :TILE]
    cols = [own[:, TILE:] * hot[j] for j in range(NOFF)]
    for n in range(BAND - 1):
        got = x_in[n].astype(F32)
        row_tot = row_tot + got[:CH]
        its_offset = off_in[n, 0:1, :]
        for j in range(NOFF):
            cols[j] = cols[j] + jnp.where(its_offset == j, got[CH:], 0.0)
    row_b = row_tot.astype(BF16)
    cols_b = [c.astype(BF16) for c in cols]
    near_part = bdot(jnp.concatenate([row_b, cols_b[0]], axis=0), emb[:, share], 1, 0)
    part_l = near_part[:CH]
    part_r = near_part[CH:] + bdot(
        jnp.concatenate(cols_b[1:], axis=1), jnp.concatenate([e_in[d] for d in range(3)], axis=0), 1, 0
    )
    mine = s_out[b]
    for c in s_c:
        c.wait_recv()
    for n in range(BAND - 1):
        mine = mine + s_in[n]
    for j in range(GROUPS):
        tail[j, 0:1] = mine[j:j + 1]
        tail[j, 1:2] = mine[8 + j:9 + j]
    for j in range(GROUPS):
        part = part_l if j < 4 else part_r
        at_j = 8 * (j % 4)
        rs_out[j] = jnp.concatenate([part[at_j:at_j + 8], tail[j]], axis=0).astype(BF16)

    g_c = [
        remote(
            rs_out.at[group_index(dy, dx)], rs_in.at[n], g_ss.at[n], g_rs.at[n], (group_at(dy, dx), b)
        )
        for n, (dy, dx) in enumerate(GROUP_OFFSETS)
    ]
    for c in g_c:
        c.start()
    for d in (1, 2, 3):
        c_out[d - 1] = cols_b[d]
    c_c = [
        remote(c_out.at[d - 1], c_in.at[d - 1], c_ss.at[d - 1], c_rs.at[d - 1], (row_at(d), b)) for d in (3, 2, 1)
    ]
    for c in c_c:
        c.start()
    mine = rs_out[g].astype(F32)
    for c in g_c:
        c.wait_recv()
    for d in range(GROUPS - 1):
        mine = mine + rs_in[d].astype(F32)
    zbuf[z] = mine.astype(BF16)

    pl.semaphore_wait(there, 2)
    z_c = [
        remote(
            zbuf.at[z], zbuf.at[z], z_ss.at[d - 1], z_rs.at[z], (ring_at(d), b)
        )
        for d in (8, 7, 9, 6, 10, 5, 11, 4, 12, 3, 13, 2, 14, 1, 15)
    ]
    for c in z_c:
        c.start()

    for c in c_c:
        c.wait_recv()
    col_tot = cols[0]
    for d in (1, 2, 3):
        col_tot = col_tot + c_in[d - 1].astype(F32)
    both_t = jnp.transpose(jnp.concatenate([row_tot, col_tot], axis=0)).astype(BF16)
    w_both = jnp.concatenate([wl[:, share], wr[:, share]], axis=0)
    gemb[...] = bdot(both_t, w_both, 1, 0).astype(BF16)

    for d in range(1, RING):
        at_z = lax.rem(z + d, RING)
        remote(zbuf.at[z], zbuf.at[at_z], z_ss.at[d - 1], z_rs.at[at_z], (ring_at(d), b)).wait_recv()
    whole = zbuf[0].astype(F32)
    for d in range(1, RING):
        whole = whole + zbuf[d].astype(F32)
    me = g * BAND + b
    fin[me] = whole.astype(BF16)

    f_c = [
        remote(fin.at[me], fin.at[me], f_ss.at[n], f_rs.at[me], (group_at(dy, dx), band_at(dh, dc)))
        for n, (dy, dx, dh, dc) in enumerate(ALL_OFFSETS)
    ]
    for c in f_c:
        c.start()
    for n, (dy, dx, dh, dc) in reversed(list(enumerate(ALL_OFFSETS))):
        src = group_index(dy, dx) * BAND + band_at(dh, dc)
        remote(
            fin.at[me], fin.at[src], f_ss.at[n], f_rs.at[src], (group_at(dy, dx), band_at(dh, dc))
        ).wait_recv()
    for j in range(GROUPS):
        out = gl if j < 4 else gr
        for e in range(BAND):
            chunk = fin[j * BAND + e].astype(F32)
            out[8 * (j % 4):8 * (j % 4) + 8, TILE * e:TILE * (e + 1)] = chunk[0:8]
            gin[8 * e + j:8 * e + j + 1, :] = chunk[8:9]
            if e == 0:
                small[j:j + 1, :] = chunk[9:10]
    ar_row = small[5:6, :] * (0.5 * ALPHA)
    gout[...] = wcol * ar_row
    ghead[...] = small[4:5, 0:CH] + bdot(
        jnp.concatenate(halves(jnp.broadcast_to(ar_row, (8, TILE))), axis=1),
        jnp.concatenate([wout[...], wout[...]], axis=1), 1, 1,
    )[0:1]
    gbias[...] = small[0:NOFF, 0:CH]

    for c in pay_c + flag_c + off_c + e_c + x_c + s_c + g_c + c_c + z_c + f_c:
        c.wait_send()


def write_out(*refs):
    n = (len(refs) - 1) // 2
    copies = [pltpu.make_async_copy(refs[i], refs[n + i], refs[-1].at[i]) for i in range(n)]
    for c in copies:
        c.start()
    for c in copies:
        c.wait()


def on_device(emb, wl, wr, win, wout, whead, dbias, offsets, vbins, target):
    def keep(x):
        return pltpu.with_memory_space_constraint(x, pltpu.HBM)

    vm = pl.BlockSpec(memory_space=pltpu.VMEM)
    hbm = pl.BlockSpec(memory_space=pltpu.HBM)
    sd = jax.ShapeDtypeStruct
    dma = pltpu.SemaphoreType.DMA
    out_shape = (
        sd((TILE, TILE), BF16), sd((TILE, TILE), BF16), sd((CH, 512), F32), sd((CH, 512), F32),
        sd((CH, HID), F32), sd((CH, HID), F32), sd((1, CH), F32), sd((NOFF, CH), F32),
    )
    outs = pl.pallas_call(
        kernel,
        out_shape=out_shape,
        in_specs=[hbm] * 7 + [pl.BlockSpec(memory_space=pltpu.SMEM)] + [hbm] * 2,
        out_specs=(vm,) * 8,
        scratch_shapes=[
            pltpu.VMEM((TILE, 512), BF16),
            pltpu.VMEM((CH, 512), BF16),
            pltpu.VMEM((CH, 512), BF16),
            pltpu.VMEM((CH, HID), BF16),
            pltpu.VMEM((CH, HID), BF16),
            pltpu.VMEM((1, CH), F32),
            pltpu.VMEM((NOFF, CH), F32),
            pltpu.VMEM((1, TILE), jnp.int32),
            pltpu.VMEM((TILE, TILE), BF16),
            dma((9,)),
            pltpu.VMEM((HID // 8, TILE, 32), BF16),
            pltpu.VMEM((16, 8 * TILE), BF16),
            pltpu.VMEM((HID, TILE, TILE), F32),
            pltpu.VMEM((HID, TILE, TILE), F32),
            pltpu.VMEM((HID, TILE), F32),
            pltpu.VMEM((HID, TILE), F32),
            pltpu.VMEM((HID, TILE), F32),
            pltpu.VMEM((HID, TILE), F32),
            pltpu.VMEM((HID, TILE), F32),
            pltpu.VMEM((CH, TILE), BF16),
            pltpu.VMEM((3, CH, TILE), BF16),
            pltpu.VMEM((16, TILE), BF16),
            pltpu.VMEM((3, 16, TILE), BF16),
            pltpu.VMEM((8, TILE), F32),
            pltpu.VMEM((3, 8, TILE), F32),
            pltpu.VMEM((3, TILE, TILE), BF16),
            pltpu.VMEM((2 * CH, TILE), BF16),
            pltpu.VMEM((3, 2 * CH, TILE), BF16),
            pltpu.VMEM((BAND, 16, TILE), F32),
            pltpu.VMEM((3, 16, TILE), F32),
            pltpu.VMEM((8, TILE), F32),
            pltpu.VMEM((GROUPS, 8, TILE), F32),
            pltpu.VMEM((GROUPS, 16, TILE), BF16),
            pltpu.VMEM((GROUPS - 1, 16, TILE), BF16),
            pltpu.VMEM((RING, 16, TILE), BF16),
            pltpu.VMEM((GROUPS * BAND, 16, TILE), BF16),
            pltpu.VMEM((3, CH, TILE), BF16),
            pltpu.VMEM((3, CH, TILE), BF16),
            dma((3,)), dma((3,)), dma((3,)), dma((3,)), dma((3,)), dma((3,)), dma((3,)), dma((3,)), dma((3,)), dma((3,)),
            dma((3,)), dma((3,)), dma((7,)), dma((7,)), dma((15,)), dma((16,)), dma((31,)), dma((32,)), dma((3,)), dma((3,)),
            pltpu.SemaphoreType.REGULAR, pltpu.SemaphoreType.REGULAR,
        ],
        compiler_params=pltpu.CompilerParams(
            collective_id=0, has_side_effects=True, vmem_limit_bytes=48 * 1024 * 1024
        ),
        name="step",
    )(
        keep(emb), keep(wl.T), keep(wr.T), keep(win), keep(wout.T), keep(whead.reshape(1, CH)), keep(dbias.T),
        offsets, keep(vbins.reshape(1, TILE)), keep(target.reshape(TILE, TILE)),
    )
    pred, gemb, gl, gr, gin, gout, ghead, gbias = pl.pallas_call(
        write_out,
        out_shape=out_shape,
        in_specs=[vm] * 8,
        out_specs=(hbm,) * 8,
        scratch_shapes=[dma((8,))],
        compiler_params=pltpu.CompilerParams(vmem_limit_bytes=1024 * 1024),
        name="write_out",
    )(*outs)
    return (
        pred.reshape(1, 1, TILE, TILE), gemb, gl.T, gr.T, gin, gout.T, ghead.reshape(CH), gbias.T,
    )


def solution(mesh):
    return jax.shard_map(
        on_device,
        mesh=mesh,
        in_specs=(
            P("rows", None), P(), P(), P(), P(), P(), P(), P("rows", "band"), P("rows"),
            P("rows", "band", None, None),
        ),
        out_specs=(P("rows", "band", None, None), P("rows", "band"), P(), P(), P(), P(), P(), P()),
        check_vma=False,
    )
```

```python
import functools

import jax
import jax.numpy as jnp
from jax import lax
from jax.experimental import pallas as pl
from jax.experimental.pallas import tpu as pltpu
from jax.sharding import PartitionSpec as P

TILE = 128
NOFF = 4
CH = 32
HID = 128
ROWS = 128
RING = 16
GROUPS = 8
BAND = 4
GROUP_OFFSETS = ((2, 1), (2, 0), (1, 1), (3, 1), (1, 0), (3, 0), (0, 1))
BAND_OFFSETS = ((1, 1), (1, 0), (0, 1))
ALL_OFFSETS = sorted(
    (
        (dy, dx, dh, dc)
        for dy in range(4) for dx in range(2) for dh in range(2) for dc in range(2)
        if dy or dx or dh or dc
    ),
    key=lambda o: (-min(o[0], 4 - o[0]) - (1 if o[1] else 2 * o[2]), -o[3]),
)
MESH = pl.DeviceIdType.MESH
F32 = jnp.float32
BF16 = jnp.bfloat16

C0 = 0.7978845608028654
C1 = C0 * 0.044715
ALPHA = C1 ** (-1.0 / 3.0)
BETA = C0 * ALPHA


def hdot(a, b, ca, cb):
    return lax.dot_general(
        a, b, (((ca,), (cb,)), ((), ())), precision=lax.Precision.HIGHEST, preferred_element_type=F32
    )


def bdot(a, b, ca, cb):
    return lax.dot_general(a, b, (((ca,), (cb,)), ((), ())), preferred_element_type=F32)


def halves(x):
    hi = x.astype(BF16)
    return hi, (x - hi.astype(F32)).astype(BF16)


def kernel(
    emb_h, wl_h, wr_h, win_h, wout_h, whead_h, dbias_h, off_h, vbins_h, tgt_h,
    pred, gemb, gl, gr, gin, gout, ghead, gbias,
    emb, wl, wr, win, wout, whead, dbias, vbins, tgt, load_s,
    lhs, spread, act, slope, b_s, v_s, gr_s, gc_s, ar_s,
    pay, pay_in, flag_out, flag_in, off_out, off_in, e_in,
    x_out, x_in, s_out, s_in, small, tail,
    rs_out, rs_in, zbuf, fin, c_out, c_in,
    pay_ss, pay_rs, flag_ss, flag_rs, off_ss, off_rs, e_ss, e_rs, x_ss, x_rs, s_ss, s_rs, g_ss, g_rs, z_ss, z_rs, f_ss, f_rs, c_ss, c_rs, here, there,
):
    r = lax.axis_index("rows")
    b = lax.axis_index("band")
    z = lax.rem(r, RING)
    base = r - z
    g = lax.div(r, RING)
    gy, gx = lax.div(g, 2), lax.rem(g, 2)
    bh, bc = lax.div(b, 2), lax.rem(b, 2)

    def row_at(d):
        return lax.rem(r + (d + ROWS), ROWS)

    def ring_at(d):
        return base + lax.rem(z + d, RING)

    def group_index(dy, dx):
        return lax.rem(gy + dy, 4) * 2 + lax.rem(gx + dx, 2)

    def group_at(dy, dx):
        return group_index(dy, dx) * RING + z

    def band_at(dh, dc):
        return lax.rem(bh + dh, 2) * 2 + lax.rem(bc + dc, 2)

    def signal(sem, dev):
        pl.semaphore_signal(sem, inc=1, device_id=dev, device_id_type=MESH)

    def remote(src, dst, ss, rs, dev):
        return pltpu.make_async_remote_copy(
            src_ref=src, dst_ref=dst, send_sem=ss, recv_sem=rs, device_id=dev, device_id_type=MESH
        )

    barrier = pltpu.get_barrier_semaphore()
    near = [(row_at(d), b) for d in (-3, 3, -2, 2, -1, 1)]
    for dev in near:
        signal(barrier, dev)
    loads = [
        pltpu.make_async_copy(src, dst, load_s.at[n])
        for n, (src, dst) in enumerate(
            [
                (wr_h, wr), (emb_h, emb), (wl_h, wl), (vbins_h, vbins), (win_h, win), (wout_h, wout),
                (whead_h, whead), (dbias_h, dbias), (tgt_h, tgt),
            ]
        )
    ]
    for c in loads:
        c.start()
    rest = [(group_at(dy, dx), b) for dy, dx in GROUP_OFFSETS]
    rest += [(r, band_at(dh, dc)) for dh, dc in BAND_OFFSETS]
    rest += [(ring_at(d), b) for d in (2, 14, 1, 15)]
    for dev in rest:
        signal(barrier, dev)

    for c in loads[:4]:
        c.wait()
    right_b = bdot(wr[...], emb[...], 1, 1).astype(BF16)
    right = right_b.astype(F32)
    flags = vbins[...].astype(F32)
    pay[...] = right_b
    flag_out[...] = jnp.broadcast_to(flags, (16, TILE)).astype(BF16)

    pl.semaphore_wait(barrier, len(near) + len(rest))
    pay_c = [
        remote(pay, pay_in.at[d - 1], pay_ss.at[d - 1], pay_rs.at[d - 1], (row_at(-d), b)) for d in (3, 2, 1)
    ]
    for c in pay_c:
        c.start()
    flag_c = [
        remote(flag_out, flag_in.at[d - 1], flag_ss.at[d - 1], flag_rs.at[d - 1], (row_at(-d), b)) for d in (3, 2, 1)
    ]
    offset = off_h[0, 0]
    off_out[...] = jnp.full((8, TILE), offset.astype(F32), F32)
    off_c = [
        remote(off_out, off_in.at[n], off_ss.at[n], off_rs.at[n], (r, band_at(dh, dc)))
        for n, (dh, dc) in enumerate(BAND_OFFSETS)
    ]
    for c in flag_c + off_c:
        c.start()
    for dy, dx in GROUP_OFFSETS:
        signal(here, (group_at(dy, dx), b))
    for d in (2, 14):
        signal(here, (ring_at(d), b))

    share = pl.ds(pl.multiple_of(b * TILE, TILE), TILE)
    left = bdot(wl[...], emb[...], 1, 1).astype(BF16).astype(F32)
    ltf = jnp.transpose(left)
    for c in loads[4:]:
        c.wait()
    wh = whead[...]
    eye = lax.broadcasted_iota(jnp.int32, (CH, CH), 0) == lax.broadcasted_iota(jnp.int32, (CH, CH), 1)
    wcol = jnp.sum(jnp.where(eye, wh, 0.0), axis=1, keepdims=True)
    wout_f = wout[...].astype(F32)
    win_f = win[...].astype(F32)
    win_t = jnp.transpose(win_f)
    v_row = jnp.sum(wout_f * wcol, axis=0, keepdims=True)
    v_s[...] = jnp.transpose(jnp.broadcast_to(v_row, (TILE, HID)))
    wcol_lin = wcol + 0.5 * jnp.sum(win_f * v_row, axis=1, keepdims=True)
    wrow_lin = jnp.sum(jnp.where(eye, wcol_lin, 0.0), axis=0, keepdims=True)
    row_logit = jnp.sum(ltf * wrow_lin, axis=1, keepdims=True)
    hot = [jnp.where(offset == j, 1.0, 0.0).astype(F32) for j in range(NOFF)]
    bias_row = sum(dbias[j:j + 1, :] * hot[j] for j in range(NOFF))
    bias_col = jnp.sum(jnp.where(eye, bias_row, 0.0), axis=1, keepdims=True)
    b_s[...] = hdot(win_t, jnp.broadcast_to(bias_col, (CH, TILE)), 1, 0) * (1.0 / ALPHA)
    row_flags = jnp.sum(
        jnp.where(
            lax.broadcasted_iota(jnp.int32, (TILE, TILE), 0) == lax.broadcasted_iota(jnp.int32, (TILE, TILE), 1),
            flags, 0.0,
        ),
        axis=1, keepdims=True,
    )
    tgt_f = tgt[...].astype(F32)
    a = bdot(win_t.astype(BF16), left.astype(BF16), 1, 0) * (1.0 / ALPHA)
    a_hi = a.astype(BF16).astype(F32)
    a_lo = a - a_hi
    ones_16 = jnp.ones((16, TILE), F32)
    for m in range(4):
        parts = []
        for i in range(4 * m, 4 * m + 4):
            parts += [a_hi[8 * i:8 * i + 8], a_lo[8 * i:8 * i + 8], ones_16]
        turned = jnp.transpose(jnp.concatenate(parts, axis=0)).astype(BF16)
        for i in range(4):
            lhs[4 * m + i] = turned[:, 32 * i:32 * i + 32]
    spread[...] = jnp.where(
        lax.rem(lax.broadcasted_iota(jnp.int32, (16, 8 * TILE), 0), 8)
        == lax.div(lax.broadcasted_iota(jnp.int32, (16, 8 * TILE), 1), TILE),
        1.0, 0.0,
    ).astype(BF16)
    tail[...] = jnp.zeros_like(tail)

    pl.semaphore_wait(here, len(GROUP_OFFSETS) + 2)
    for d in (4, 12):
        signal(there, (ring_at(d), b))

    weight = [hot[0]] + [hot[d] * jnp.where(r + d < ROWS, 1.0, 0.0).astype(F32) for d in (1, 2, 3)]
    r_sel = right * weight[0]
    for c in pay_c:
        c.wait_recv()
    for d in (1, 2, 3):
        r_sel = r_sel + pay_in[d - 1].astype(F32) * weight[d]

    e_c = [
        remote(emb.at[:, share], e_in.at[d - 1], e_ss.at[d - 1], e_rs.at[d - 1], (row_at(-d), b)) for d in (3, 2, 1)
    ]
    for c in e_c:
        c.start()

    r_b = r_sel + bias_col
    b_s[...] += bdot(win_t.astype(BF16), r_sel.astype(BF16), 1, 0) * (1.0 / ALPHA)
    col_logit = jnp.sum(r_b * wcol_lin, axis=0, keepdims=True)
    p_hi, p_lo = halves(jnp.concatenate([left, r_b], axis=1))
    p_3 = jnp.concatenate([p_hi, p_hi, p_lo], axis=1)

    def first(i, total):
        b8 = b_s[pl.ds(pl.multiple_of(8 * i, 8), 8), :]
        b_hi = b8.astype(BF16).astype(F32)
        b_16 = jnp.concatenate([b_hi, b8 - b_hi], axis=0).astype(BF16)
        mask = spread[...]
        rhs = jnp.concatenate([mask, jnp.concatenate([b_16] * 8, axis=1) * mask], axis=0)
        y_8 = bdot(lhs[i], rhs, 1, 0)
        for j in range(8):
            k = 8 * i + j
            y = y_8[:, TILE * j:TILE * (j + 1)]
            w = y * y + BETA
            t = jnp.tanh(y * w)
            yt = y * t
            act[k] = yt
            slope[k] = t + (y - t * yt) * (3.0 * w - 2.0 * BETA)
            total = total + yt * v_s[pl.ds(k, 1), :]
        return total

    total = lax.fori_loop(0, HID // 8, first, jnp.zeros((TILE, TILE), F32), unroll=4)
    logits = total * (0.5 * ALPHA) + (row_logit + col_logit)
    pred[...] = logits.astype(BF16)
    f_sel = flags * weight[0]
    for c in flag_c:
        c.wait_recv()
    for d in (1, 2, 3):
        f_sel = f_sel + flag_in[d - 1].astype(F32)[0:1] * weight[d]
    res = (row_flags * f_sel) * (logits - tgt_f) * (1.0 / (NOFF * TILE))
    ones = jnp.ones((8, TILE), BF16)

    res_hi, res_lo = halves(res)
    rr = bdot(jnp.ones((8, 2 * TILE), BF16), jnp.concatenate([res_hi, res_lo], axis=1), 1, 1)
    rc = jnp.broadcast_to(jnp.sum(res, axis=0, keepdims=True), (8, TILE))
    r_both = jnp.concatenate([rr, rc], axis=1)
    half_v = v_s[...] * 0.5
    parts = []
    for k in range(HID):
        h = slope[k] * res
        gc_s[k:k + 1, :] = jnp.sum(h, axis=0, keepdims=True)
        ar_s[k:k + 1, :] = jnp.sum(act[k] * res, axis=0, keepdims=True)
        parts.append(h.astype(BF16))
    over_q = bdot(ones, jnp.concatenate(parts, axis=0), 1, 1)
    for k in range(HID):
        gr_s[k:k + 1, :] = over_q[0:1, TILE * k:TILE * (k + 1)]

    g_both = jnp.concatenate([(gr_s[...] + rr[0:1]) * half_v, (gc_s[...] + rc[0:1]) * half_v], axis=1)
    g_hi, g_lo = halves(g_both)
    sums = wcol * r_both[0:1] + bdot(
        jnp.concatenate([win[...], win[...]], axis=1), jnp.concatenate([g_hi, g_lo], axis=0), 1, 0
    )
    sums_b = sums.astype(BF16)

    x_out[0:CH] = sums_b[:, :TILE]
    x_out[CH:2 * CH] = sums_b[:, TILE:]
    x_c, s_c = [], []
    for n, (dh, dc) in enumerate(BAND_OFFSETS):
        dev = (r, band_at(dh, dc))
        x_c.append(remote(x_out, x_in.at[n], x_ss.at[n], x_rs.at[n], dev))
        s_c.append(remote(s_out.at[band_at(dh, dc)], s_in.at[n], s_ss.at[n], s_rs.at[n], dev))
    for c in x_c:
        c.start()
    r_hi, r_lo = halves(r_both)
    gin_part = bdot(p_3, jnp.concatenate([g_hi, g_lo, g_hi], axis=1), 1, 1)
    head = bdot(jnp.concatenate([r_hi, r_lo, r_hi], axis=1), p_3, 1, 1)
    ones_2 = jnp.ones((8, 2 * TILE), BF16)
    bias = bdot(ones_2, jnp.concatenate(halves(sums[:, :TILE]), axis=1), 1, 1)
    h_hi, h_lo = halves(head)
    ar = bdot(ones_2, jnp.concatenate(halves(ar_s[...]), axis=1), 1, 1) + bdot(
        jnp.concatenate([h_hi, h_lo], axis=1), jnp.concatenate([win[...], win[...]], axis=0), 1, 0
    ) * (1.0 / ALPHA)
    row_id = lax.broadcasted_iota(jnp.int32, (8, TILE), 0)
    small[...] = jnp.where(row_id == 5, ar, 0.0)
    for j in range(NOFF):
        small[j:j + 1, 0:CH] = bias[0:1] * hot[j]
    small[4:5, 0:CH] = head[0:1]
    extra = small[...]
    for e in range(BAND):
        s_out[e, 0:8] = gin_part[8 * e:8 * e + 8]
        s_out[e, 8:16] = extra
    for c in s_c:
        c.start()
    for c in e_c + off_c + x_c:
        c.wait_recv()
    own = sums_b.astype(F32)
    row_tot = own[:, :TILE]
    cols = [own[:, TILE:] * hot[j] for j in range(NOFF)]
    for n in range(BAND - 1):
        got = x_in[n].astype(F32)
        row_tot = row_tot + got[:CH]
        its_offset = off_in[n, 0:1, :]
        for j in range(NOFF):
            cols[j] = cols[j] + jnp.where(its_offset == j, got[CH:], 0.0)
    row_b = row_tot.astype(BF16)
    cols_b = [c.astype(BF16) for c in cols]
    near_part = bdot(jnp.concatenate([row_b, cols_b[0]], axis=0), emb[:, share], 1, 0)
    part_l = near_part[:CH]
    part_r = near_part[CH:] + bdot(
        jnp.concatenate(cols_b[1:], axis=1), jnp.concatenate([e_in[d] for d in range(3)], axis=0), 1, 0
    )
    mine = s_out[b]
    for c in s_c:
        c.wait_recv()
    for n in range(BAND - 1):
        mine = mine + s_in[n]
    for j in range(GROUPS):
        tail[j, 0:1] = mine[j:j + 1]
        tail[j, 1:2] = mine[8 + j:9 + j]
    for j in range(GROUPS):
        part = part_l if j < 4 else part_r
        at_j = 8 * (j % 4)
        rs_out[j] = jnp.concatenate([part[at_j:at_j + 8], tail[j]], axis=0).astype(BF16)

    g_c = [
        remote(
            rs_out.at[group_index(dy, dx)], rs_in.at[n], g_ss.at[n], g_rs.at[n], (group_at(dy, dx), b)
        )
        for n, (dy, dx) in enumerate(GROUP_OFFSETS)
    ]
    for c in g_c:
        c.start()
    for d in (1, 2, 3):
        c_out[d - 1] = cols_b[d]
    c_c = [
        remote(c_out.at[d - 1], c_in.at[d - 1], c_ss.at[d - 1], c_rs.at[d - 1], (row_at(d), b)) for d in (3, 2, 1)
    ]
    for c in c_c:
        c.start()
    mine = rs_out[g].astype(F32)
    for c in g_c:
        c.wait_recv()
    for d in range(GROUPS - 1):
        mine = mine + rs_in[d].astype(F32)
    zbuf[z] = mine.astype(BF16)

    pl.semaphore_wait(there, 2)
    z_c = [
        remote(
            zbuf.at[z], zbuf.at[z], z_ss.at[d - 1], z_rs.at[z], (ring_at(d), b)
        )
        for d in (8, 7, 9, 6, 10, 5, 11, 4, 12, 3, 13, 2, 14, 1, 15)
    ]
    for c in z_c:
        c.start()

    for c in c_c:
        c.wait_recv()
    col_tot = cols[0]
    for d in (1, 2, 3):
        col_tot = col_tot + c_in[d - 1].astype(F32)
    both_t = jnp.transpose(jnp.concatenate([row_tot, col_tot], axis=0)).astype(BF16)
    w_both = jnp.concatenate([wl[:, share], wr[:, share]], axis=0)
    gemb[...] = bdot(both_t, w_both, 1, 0).astype(BF16)

    for d in range(1, RING):
        at_z = lax.rem(z + d, RING)
        remote(zbuf.at[z], zbuf.at[at_z], z_ss.at[d - 1], z_rs.at[at_z], (ring_at(d), b)).wait_recv()
    whole = zbuf[0].astype(F32)
    for d in range(1, RING):
        whole = whole + zbuf[d].astype(F32)
    me = g * BAND + b
    fin[me] = whole.astype(BF16)

    f_c = [
        remote(fin.at[me], fin.at[me], f_ss.at[n], f_rs.at[me], (group_at(dy, dx), band_at(dh, dc)))
        for n, (dy, dx, dh, dc) in enumerate(ALL_OFFSETS)
    ]
    for c in f_c:
        c.start()
    for n, (dy, dx, dh, dc) in reversed(list(enumerate(ALL_OFFSETS))):
        src = group_index(dy, dx) * BAND + band_at(dh, dc)
        remote(
            fin.at[me], fin.at[src], f_ss.at[n], f_rs.at[src], (group_at(dy, dx), band_at(dh, dc))
        ).wait_recv()
    for j in range(GROUPS):
        out = gl if j < 4 else gr
        for e in range(BAND):
            chunk = fin[j * BAND + e].astype(F32)
            out[8 * (j % 4):8 * (j % 4) + 8, TILE * e:TILE * (e + 1)] = chunk[0:8]
            gin[8 * e + j:8 * e + j + 1, :] = chunk[8:9]
            if e == 0:
                small[j:j + 1, :] = chunk[9:10]
    ar_row = small[5:6, :] * (0.5 * ALPHA)
    gout[...] = wcol * ar_row
    ghead[...] = small[4:5, 0:CH] + bdot(
        jnp.concatenate(halves(jnp.broadcast_to(ar_row, (8, TILE))), axis=1),
        jnp.concatenate([wout[...], wout[...]], axis=1), 1, 1,
    )[0:1]
    gbias[...] = small[0:NOFF, 0:CH]

    for c in pay_c + flag_c + off_c + e_c + x_c + s_c + g_c + c_c + z_c + f_c:
        c.wait_send()


def write_out(*refs):
    n = (len(refs) - 1) // 2
    copies = [pltpu.make_async_copy(refs[i], refs[n + i], refs[-1].at[i]) for i in range(n)]
    for c in copies:
        c.start()
    for c in copies:
        c.wait()


def on_device(emb, wl, wr, win, wout, whead, dbias, offsets, vbins, target):
    def keep(x):
        return pltpu.with_memory_space_constraint(x, pltpu.HBM)

    vm = pl.BlockSpec(memory_space=pltpu.VMEM)
    hbm = pl.BlockSpec(memory_space=pltpu.HBM)
    sd = jax.ShapeDtypeStruct
    dma = pltpu.SemaphoreType.DMA
    out_shape = (
        sd((TILE, TILE), BF16), sd((TILE, TILE), BF16), sd((CH, 512), F32), sd((CH, 512), F32),
        sd((CH, HID), F32), sd((CH, HID), F32), sd((1, CH), F32), sd((NOFF, CH), F32),
    )
    outs = pl.pallas_call(
        kernel,
        out_shape=out_shape,
        in_specs=[hbm] * 7 + [pl.BlockSpec(memory_space=pltpu.SMEM)] + [hbm] * 2,
        out_specs=(vm,) * 8,
        scratch_shapes=[
            pltpu.VMEM((TILE, 512), BF16),
            pltpu.VMEM((CH, 512), BF16),
            pltpu.VMEM((CH, 512), BF16),
            pltpu.VMEM((CH, HID), BF16),
            pltpu.VMEM((CH, HID), BF16),
            pltpu.VMEM((1, CH), F32),
            pltpu.VMEM((NOFF, CH), F32),
            pltpu.VMEM((1, TILE), jnp.int32),
            pltpu.VMEM((TILE, TILE), BF16),
            dma((9,)),
            pltpu.VMEM((HID // 8, TILE, 32), BF16),
            pltpu.VMEM((16, 8 * TILE), BF16),
            pltpu.VMEM((HID, TILE, TILE), F32),
            pltpu.VMEM((HID, TILE, TILE), F32),
            pltpu.VMEM((HID, TILE), F32),
            pltpu.VMEM((HID, TILE), F32),
            pltpu.VMEM((HID, TILE), F32),
            pltpu.VMEM((HID, TILE), F32),
            pltpu.VMEM((HID, TILE), F32),
            pltpu.VMEM((CH, TILE), BF16),
            pltpu.VMEM((3, CH, TILE), BF16),
            pltpu.VMEM((16, TILE), BF16),
            pltpu.VMEM((3, 16, TILE), BF16),
            pltpu.VMEM((8, TILE), F32),
            pltpu.VMEM((3, 8, TILE), F32),
            pltpu.VMEM((3, TILE, TILE), BF16),
            pltpu.VMEM((2 * CH, TILE), BF16),
            pltpu.VMEM((3, 2 * CH, TILE), BF16),
            pltpu.VMEM((BAND, 16, TILE), F32),
            pltpu.VMEM((3, 16, TILE), F32),
            pltpu.VMEM((8, TILE), F32),
            pltpu.VMEM((GROUPS, 8, TILE), F32),
            pltpu.VMEM((GROUPS, 16, TILE), BF16),
            pltpu.VMEM((GROUPS - 1, 16, TILE), BF16),
            pltpu.VMEM((RING, 16, TILE), BF16),
            pltpu.VMEM((GROUPS * BAND, 16, TILE), BF16),
            pltpu.VMEM((3, CH, TILE), BF16),
            pltpu.VMEM((3, CH, TILE), BF16),
            dma((3,)), dma((3,)), dma((3,)), dma((3,)), dma((3,)), dma((3,)), dma((3,)), dma((3,)), dma((3,)), dma((3,)),
            dma((3,)), dma((3,)), dma((7,)), dma((7,)), dma((15,)), dma((16,)), dma((31,)), dma((32,)), dma((3,)), dma((3,)),
            pltpu.SemaphoreType.REGULAR, pltpu.SemaphoreType.REGULAR,
        ],
        compiler_params=pltpu.CompilerParams(
            collective_id=0, has_side_effects=True, vmem_limit_bytes=48 * 1024 * 1024
        ),
        name="step",
    )(
        keep(emb), keep(wl.T), keep(wr.T), keep(win), keep(wout.T), keep(whead.reshape(1, CH)), keep(dbias.T),
        offsets, keep(vbins.reshape(1, TILE)), keep(target.reshape(TILE, TILE)),
    )
    pred, gemb, gl, gr, gin, gout, ghead, gbias = pl.pallas_call(
        write_out,
        out_shape=out_shape,
        in_specs=[vm] * 8,
        out_specs=(hbm,) * 8,
        scratch_shapes=[dma((8,))],
        compiler_params=pltpu.CompilerParams(vmem_limit_bytes=1024 * 1024),
        name="write_out",
    )(*outs)
    return (
        pred.reshape(1, 1, TILE, TILE), gemb, gl.T, gr.T, gin, gout.T, ghead.reshape(CH), gbias.T,
    )


def solution(mesh):
    return jax.shard_map(
        on_device,
        mesh=mesh,
        in_specs=(
            P("rows", None), P(), P(), P(), P(), P(), P(), P("rows", "band"), P("rows"),
            P("rows", "band", None, None),
        ),
        out_specs=(P("rows", "band", None, None), P("rows", "band"), P(), P(), P(), P(), P(), P()),
        check_vma=False,
    )
```
